32 devices in a mesh: sens: 4 (over y, x), pts: 8 (over z, core).
Axes of the slice: x: 2, y: 2, z: 4, core: 2. Of those that a mesh axis runs over, the one named last changes fastest.
Arguments:
- vectors: float32 [4, 256, 420], P(None, 'pts'), may hold values from -6 to 6
- kernel_hat: float32 [2, 424, 256, 256], P(None, 'pts', 'sens'), may hold values from -0.375 to 0.375
- noise_prec: float32 [256], P(('sens', 'pts')), may hold values from 0.3 to 3
- stencil_coefficients_raw: float32 [256, 6], P('pts'), may hold values from 0.1 to 2
- offsets: int32 [256, 6], P('pts'), may hold values from -32 to 32
- amplitude: float32 [256], P('pts'), may hold values from 0.5 to 2
- cheb_coef: float32 [5], replicated, may hold values from 0.2 to 1
Outputs:
- hess_vec: float32 [4, 256, 420], P(None, 'pts')
The draws below stay inside these ranges and needn't reach their ends.
Inputs may be any that keep to these rules, and one draw needn't show every extreme that they name: `offsets`: each point's stencil neighbours lie at most 32 points away in the point order.
All inputs are finite; a program needn't handle non-finite values.
Results may differ from the reference program's by a relative error of at most 0.00016.
Values sent between devices are 32-bit elements; how exact they have to be, the bound alone decides.
A program may use at most 64 MiB of HBM per device.

```python
import math
import jax
import jax.numpy as jnp
from jax import lax

NT = 420
NV = 4
DEG = 4
NB = 6
PTS_DEV = 32
PTS = 256
SENSORS = 256
NFP = 424


def place_ends(values, key, smallest, largest):
    shape = values.shape
    index_at = [jax.random.randint(jax.random.fold_in(key, axis), (), 0, shape[axis]) for axis in range(len(shape))]
    values = values.at[tuple(index_at)].set(smallest)
    longest = shape.index(max(shape))
    index_at[longest] = (index_at[longest] + 1) % shape[longest]
    return values.at[tuple(index_at)].set(largest)


def block_levels(rng, extent, cuts, smallest, high):
    def one(axis_at, parts):
        draws = jax.random.uniform(jax.random.fold_in(jax.random.fold_in(rng, 6), axis_at), (parts,), jnp.float32, smallest / len(cuts), high / len(cuts))
        return jnp.repeat(jnp.exp(draws), extent[axis_at] // parts).reshape((-1,) + (1,) * (len(extent) - axis_at - 1))

    factor_of = one(*cuts[0])
    for cut in cuts[1:]:
        factor_of = factor_of * one(*cut)
    return factor_of


def scatter_about(key, extent, scale, bound, cuts=(), kind=jnp.bfloat16):
    level = block_levels(key, extent, cuts, -0.22, 0.18) if cuts else 1.0
    entries = jax.random.normal(key, extent, jnp.float32) * scale * level
    return jnp.minimum(jnp.maximum(entries, -bound), bound).astype(kind)


def setup_inputs(seed: int = 0) -> dict:
    keys = jax.random.split(jax.random.key(seed), 8)
    vectors = scatter_about(keys[0], (NV, PTS, NT), 1.0, 6.0, ((1, 8),), jnp.float32)
    kernel_hat = scatter_about(keys[1], (2, NFP, SENSORS, PTS), PTS ** -0.5, 0.375, ((1, 8), (2, 4)), jnp.float32)
    noise_prec = jnp.clip(jnp.exp(math.log(3.0) - 2.3025851 * jax.random.uniform(keys[2], (SENSORS,), jnp.float32) ** block_levels(keys[2], (SENSORS,), ((0, 32),), -0.2, 0.2)), 0.3, 3.0)
    stencil_coefficients_raw = jnp.clip(jnp.exp(math.log(2.0) - 2.9957323 * jax.random.uniform(keys[3], (PTS, NB), jnp.float32) ** block_levels(keys[3], (PTS, NB), ((0, 8),), -0.2, 0.2)), 0.1, 2.0)
    offsets = place_ends(jax.random.randint(keys[4], (PTS, NB), 0 - PTS_DEV, PTS_DEV + 1), jax.random.fold_in(keys[4], 1), 0 - PTS_DEV, PTS_DEV).astype(jnp.int32)
    amplitude = jnp.clip(jnp.exp(math.log(2.0) - 1.3862944 * jax.random.uniform(keys[5], (PTS,), jnp.float32) ** block_levels(keys[5], (PTS,), ((0, 8),), -0.2, 0.2)), 0.5, 2.0)
    cheb_coef = jnp.clip(jnp.exp(jax.random.uniform(keys[6], (DEG + 1,), jnp.float32, math.log(0.2), math.log(1.0))), 0.2, 1.0)
    return dict(vectors=vectors, kernel_hat=kernel_hat, noise_prec=noise_prec, stencil_coefficients_raw=stencil_coefficients_raw, offsets=offsets, amplitude=amplitude, cheb_coef=cheb_coef)


def stencil_parts(point_count, stencil_coefficients_raw, offsets):
    weights = stencil_coefficients_raw / jnp.sum(stencil_coefficients_raw, axis=1, keepdims=True)
    target = jnp.arange(point_count, dtype=jnp.int32)[:, None] + offsets
    inside = (target >= 0) & (target < point_count)
    weights = jnp.where(inside, weights, jnp.zeros_like(weights))
    clipped = jnp.clip(target, 0, point_count - 1).astype(jnp.int32)
    return weights, clipped


def chebyshev(values_in, operator, cheb_coef):
    previous = values_in
    current = operator(values_in)
    running_sum = cheb_coef[0] * previous + cheb_coef[1] * current
    for degree in range(2, DEG + 1):
        following = 2.0 * operator(current) - previous
        previous, current = current, following
        running_sum = running_sum + cheb_coef[degree] * current
    return running_sum


def prior_operator_apply(values_in, stencil_coefficients_raw, offsets, amplitude, cheb_coef):
    weights, clipped = stencil_parts(values_in.shape[1], stencil_coefficients_raw, offsets)

    def neighbour_mean(values):
        picked = jnp.take(values, clipped, axis=1)
        return jnp.sum(weights[None, :, :, None] * picked, axis=2)

    return amplitude[None, :, None] * chebyshev(values_in, neighbour_mean, cheb_coef)


def apply_prior_transposed(values_in, stencil_coefficients_raw, offsets, amplitude, cheb_coef):
    weights, clipped = stencil_parts(values_in.shape[1], stencil_coefficients_raw, offsets)

    def spread_back(values):
        contrib = weights[None, :, :, None] * values[:, :, None, :]
        return jnp.zeros_like(values).at[:, clipped].add(contrib)

    return chebyshev(amplitude[None, :, None] * values_in, spread_back, cheb_coef)


def reference(vectors, kernel_hat, noise_prec, stencil_coefficients_raw, offsets, amplitude, cheb_coef):
    exact_evaluation_flag = lax.Precision.HIGHEST
    frequency_total_count = NT + 1
    prior_field = prior_operator_apply(vectors, stencil_coefficients_raw, offsets, amplitude, cheb_coef)
    spectrum = jnp.fft.rfft(prior_field, n=2 * NT, axis=2)
    spectrum_real = jnp.transpose(spectrum.real, (2, 0, 1))
    spectrum_imag = jnp.transpose(spectrum.imag, (2, 0, 1))
    freq_index = jnp.arange(frequency_total_count, dtype=jnp.int32)

    def forward_one(items):
        index_now, real_part, imag_part = items
        kernel_rows = lax.dynamic_index_in_dim(kernel_hat, index_now, 1, keepdims=False)
        kernel_real, kernel_imag = kernel_rows[0], kernel_rows[1]
        data_real = jnp.dot(real_part, kernel_real.T, precision=exact_evaluation_flag) - jnp.dot(imag_part, kernel_imag.T, precision=exact_evaluation_flag)
        data_imag = jnp.dot(imag_part, kernel_real.T, precision=exact_evaluation_flag) + jnp.dot(real_part, kernel_imag.T, precision=exact_evaluation_flag)
        return data_real, data_imag

    data_real, data_imag = lax.map(forward_one, (freq_index, spectrum_real, spectrum_imag))
    data_spec = jnp.transpose(data_real, (1, 2, 0)) + 1j * jnp.transpose(data_imag, (1, 2, 0))
    data = jnp.fft.irfft(data_spec, n=2 * NT, axis=2)[:, :, :NT] * noise_prec[None, :, None]
    data_back = jnp.fft.rfft(data, n=2 * NT, axis=2)
    back_real = jnp.transpose(data_back.real, (2, 0, 1))
    back_imag = jnp.transpose(data_back.imag, (2, 0, 1))

    def adjoint_one(items):
        index_now, real_part, imag_part = items
        kernel_rows = lax.dynamic_index_in_dim(kernel_hat, index_now, 1, keepdims=False)
        kernel_real, kernel_imag = kernel_rows[0], kernel_rows[1]
        grad_real = jnp.dot(real_part, kernel_real, precision=exact_evaluation_flag) + jnp.dot(imag_part, kernel_imag, precision=exact_evaluation_flag)
        grad_imag = jnp.dot(imag_part, kernel_real, precision=exact_evaluation_flag) - jnp.dot(real_part, kernel_imag, precision=exact_evaluation_flag)
        return grad_real, grad_imag

    grad_real, grad_imag = lax.map(adjoint_one, (freq_index, back_real, back_imag))
    grad_spec = jnp.transpose(grad_real, (1, 2, 0)) + 1j * jnp.transpose(grad_imag, (1, 2, 0))
    gradient = jnp.fft.irfft(grad_spec, n=2 * NT, axis=2)[:, :, :NT]
    return vectors + apply_prior_transposed(gradient, stencil_coefficients_raw, offsets, amplitude, cheb_coef)
```

```python
import functools

import jax
import jax.numpy as jnp
import ml_dtypes
import numpy as np
from jax import lax
from jax.experimental import pallas as pl
from jax.experimental.pallas import tpu as pltpu
from jax.sharding import PartitionSpec as P

exact_evaluation_flag = lax.Precision.HIGHEST


def transform_tables(length, padded):
    time_index = jnp.arange(length, dtype=jnp.int32)
    frequency = jnp.arange(padded, dtype=jnp.int32)
    period = 2 * length
    phase_index = frequency[:, None] * time_index[None, :] % period
    angles = 2.0 * jnp.pi / period * phase_index.astype(jnp.float32)
    active = (frequency <= length).astype(jnp.float32)[:, None]
    cosine = jnp.cos(angles)
    sine_part = jnp.sin(angles)
    forward_operator = jnp.stack([cosine * active, -sine_part * active])
    edge_rows = (frequency == 0) | (frequency == length)
    weight = jnp.where(edge_rows, 1.0, 2.0).astype(jnp.float32)[:, None] * active / period
    inverse = jnp.stack([cosine * weight, -sine_part * weight])
    return (forward_operator, inverse)


def to_spectrum(time_series_values, forward_operator):
    return jnp.einsum(
        "vpt,cft->vcfp", time_series_values, forward_operator, precision=exact_evaluation_flag
    )


def to_series(spectrum, inverse):
    return jnp.einsum("vcfp,cft->vpt", spectrum, inverse, precision=exact_evaluation_flag)


def chebyshev(values_in, operator, cheb_coef):
    previous = values_in
    current = operator(values_in)
    running_sum = cheb_coef[0] * previous + cheb_coef[1] * current
    for degree in range(2, cheb_coef.shape[0]):
        following = 2.0 * operator(current) - previous
        previous, current = (current, following)
        running_sum = running_sum + cheb_coef[degree] * current
    return running_sum


def full_matrix(weights_all, offsets_all):
    point_count = weights_all.shape[0]
    positions = jnp.arange(point_count, dtype=jnp.int32)
    target = positions[:, None] + offsets_all
    dense_operator_matrix = jnp.zeros((point_count, point_count), jnp.float32)
    for column in range(weights_all.shape[1]):
        hit = (target[:, column][:, None] == positions[None, :]).astype(jnp.float32)
        dense_operator_matrix = dense_operator_matrix + weights_all[:, column][:, None] * hit
    return dense_operator_matrix


def plain(vectors, kernel_hat, noise_prec, stencil_coefficients_raw, offsets, amplitude, cheb_coef):
    length = vectors.shape[2]
    freq_block = kernel_hat.shape[1]
    padded = freq_block * lax.axis_size("pts")
    forward_operator, inverse = transform_tables(length, padded)
    weights = stencil_coefficients_raw / jnp.sum(stencil_coefficients_raw, axis=1, keepdims=True)
    kernel_real = kernel_hat[0]
    kernel_imag = kernel_hat[1]
    offsets_all = lax.all_gather(offsets, "pts", axis=0, tiled=True)
    weights_all, amplitude_all = (
        lax.all_gather(weights, "pts", axis=0, tiled=True),
        lax.all_gather(amplitude, "pts", axis=0, tiled=True),
    )
    dense_operator_matrix = full_matrix(weights_all, offsets_all)

    def forward_mean(values):
        return jnp.einsum(
            "vcfq,pq->vcfp", values, dense_operator_matrix, precision=exact_evaluation_flag
        )

    def backward_mean(values):
        return jnp.einsum(
            "vcfp,pq->vcfq", values, dense_operator_matrix, precision=exact_evaluation_flag
        )

    source = to_spectrum(vectors, forward_operator)
    spectrum = lax.all_to_all(source, "pts", split_axis=2, concat_axis=3, tiled=True)
    spectrum = amplitude_all[None, None, None, :] * chebyshev(spectrum, forward_mean, cheb_coef)
    real_part = spectrum[:, 0]
    imag_part = spectrum[:, 1]
    data_real = jnp.einsum(
        "fsp,vfp->vfs", kernel_real, real_part, precision=exact_evaluation_flag
    ) - jnp.einsum("fsp,vfp->vfs", kernel_imag, imag_part, precision=exact_evaluation_flag)
    data_imag = jnp.einsum(
        "fsp,vfp->vfs", kernel_real, imag_part, precision=exact_evaluation_flag
    ) + jnp.einsum("fsp,vfp->vfs", kernel_imag, real_part, precision=exact_evaluation_flag)
    data_spec = jnp.stack([data_real, data_imag], axis=1)
    time_series_values = (
        jnp.einsum(
            "rklu,klq->ruq",
            lax.all_to_all(data_spec, "pts", split_axis=3, concat_axis=2, tiled=True),
            inverse,
            precision=exact_evaluation_flag,
        )
        * noise_prec[None, :, None]
    )
    weighted_result = jnp.einsum(
        "lew,jkw->ljke", time_series_values, forward_operator, precision=exact_evaluation_flag
    )
    weighted_result = lax.all_to_all(
        weighted_result, "pts", split_axis=2, concat_axis=3, tiled=True
    )
    back_real = weighted_result[:, 0]
    back_imag = weighted_result[:, 1]
    grad_real = jnp.einsum(
        "fsp,vfs->vfp", kernel_real, back_real, precision=exact_evaluation_flag
    ) + jnp.einsum("fsp,vfs->vfp", kernel_imag, back_imag, precision=exact_evaluation_flag)
    grad_imag = jnp.einsum(
        "fsp,vfs->vfp", kernel_real, back_imag, precision=exact_evaluation_flag
    ) - jnp.einsum("fsp,vfs->vfp", kernel_imag, back_real, precision=exact_evaluation_flag)
    partial_value = chebyshev(
        amplitude_all[None, None, None, :] * jnp.stack([grad_real, grad_imag], axis=1),
        backward_mean,
        cheb_coef,
    )
    summed = lax.psum(partial_value, "sens")
    moved = lax.all_to_all(summed, "pts", split_axis=3, concat_axis=2, tiled=True)
    gradient = to_series(moved, inverse)
    return vectors + gradient


BF = jnp.bfloat16
F32 = jnp.float32
MESH = pl.DeviceIdType.MESH


def up(size, multiple):
    return -(-size // multiple) * multiple


def host_tables(length, block, blocks, padded_block, lanes, padded_time):
    period = 2 * length
    forward = np.zeros((padded_time, blocks, lanes))
    inverse = np.zeros((blocks, lanes, padded_time))
    time = np.arange(length)
    for index in range(blocks):
        frequency = index * block + np.arange(block)
        angle = 2.0 * np.pi / period * (frequency[:, None] * time[None, :] % period)
        active = (frequency <= length)[:, None]
        edge = (frequency == 0) | (frequency == length)
        weight = np.where(edge, 1.0, 2.0)[:, None] / period
        for part, table in enumerate((np.cos(angle) * active, -np.sin(angle) * active)):
            at = slice(part * padded_block, part * padded_block + block)
            forward[:length, index, at] = table.T
            inverse[index, at, :length] = table * weight
    halves = []
    for table in (forward.reshape(padded_time, -1), inverse.reshape(-1, padded_time)):
        high = table.astype(ml_dtypes.bfloat16)
        low = (table - high.astype(np.float64)).astype(ml_dtypes.bfloat16)
        halves.append(np.stack([high, low]))
    return halves


def split(values):
    high = values.astype(BF)
    return high, (values - high.astype(F32)).astype(BF)


NN = (((1,), (0,)), ((), ()))
NT = (((1,), (1,)), ((), ()))


def dot3(left, right_high, right_low, dims=NN):
    rows = left.shape[0]
    high, low = split(left)
    both = lax.dot_general(
        jnp.concatenate([high, low], axis=0), right_high, dims, preferred_element_type=F32
    )
    cross = lax.dot_general(high, right_low, dims, preferred_element_type=F32)
    return both[:rows] + both[rows:] + cross


def fused_kernel(
    sizes,
    vec, kern, noise, raw, offs, amp, cheb, fwd_in, inv_in,
    out,
    fwd, inv, k_f32, k_hl, v_pad, pack, a_send, a_recv, spec, y_buf, d_send, d_recv,
    e_send, e_recv, l_buf, g_buf, r_recv, h_send, h_recv, o_buf,
    load_sem, pack_s, pack_r, a_s, a_r, s_s, s_r, d_s, d_r, e_s, e_r, g_s, g_r, h_s, h_r, o_s, o_r,
):
    nv, n_sens, n_pts, fb, fbp, cfp, sl, sq, pt, ple, length, tp = sizes
    me_s = lax.axis_index("sens")
    me_p = lax.axis_index("pts")
    rows = 2 * nv

    loads = [
        pltpu.make_async_copy(fwd_in, fwd, load_sem.at[0]),
        pltpu.make_async_copy(kern.at[0], k_f32.at[0], load_sem.at[1]),
        pltpu.make_async_copy(kern.at[1], k_f32.at[1], load_sem.at[2]),
        pltpu.make_async_copy(inv_in, inv, load_sem.at[3]),
    ]
    for load in loads:
        load.start()

    barrier = pltpu.get_barrier_semaphore()
    for step in range(1, n_pts):
        pl.semaphore_signal(
            barrier, inc=1, device_id=(me_s, lax.rem(me_p + step, n_pts)), device_id_type=MESH
        )
    for step in range(1, n_sens):
        pl.semaphore_signal(
            barrier, inc=1, device_id=(lax.rem(me_s + step, n_sens), me_p), device_id_type=MESH
        )

    def over_pts(step, src, dst, send_sem, recv_sem):
        target = lax.rem(me_p + step, n_pts)
        return pltpu.make_async_remote_copy(
            src_ref=src(target), dst_ref=dst(me_p), send_sem=send_sem.at[step],
            recv_sem=recv_sem.at[step], device_id=(me_s, target), device_id_type=MESH,
        )

    def over_sens(step, src, dst, send_sem, recv_sem):
        target = lax.rem(me_s + step, n_sens)
        return pltpu.make_async_remote_copy(
            src_ref=src(target), dst_ref=dst(me_s), send_sem=send_sem.at[step],
            recv_sem=recv_sem.at[step], device_id=(target, me_p), device_id_type=MESH,
        )

    def arrive_pts(step, src, dst, send_sem, recv_sem):
        source = lax.rem(me_p - step + n_pts, n_pts)
        pltpu.make_async_remote_copy(
            src_ref=src(source), dst_ref=dst(source), send_sem=send_sem.at[step],
            recv_sem=recv_sem.at[step], device_id=(me_s, source), device_id_type=MESH,
        ).wait_recv()

    def arrive_sens(step, src, dst, send_sem, recv_sem):
        source = lax.rem(me_s - step + n_sens, n_sens)
        pltpu.make_async_remote_copy(
            src_ref=src(source), dst_ref=dst(source), send_sem=send_sem.at[step],
            recv_sem=recv_sem.at[step], device_id=(source, me_p), device_id_type=MESH,
        ).wait_recv()

    pts_steps = range(1, n_pts)
    sens_steps = range(1, n_sens)
    started = []

    def send_pts(*args):
        for step in pts_steps:
            copy = over_pts(step, *args)
            copy.start()
            started.append(copy)

    def send_sens(*args):
        for step in sens_steps:
            copy = over_sens(step, *args)
            copy.start()
            started.append(copy)

    nb = raw.shape[1]
    pack[me_p] = jnp.zeros(pack.shape[1:], F32)
    raw_t = jnp.transpose(raw[...])
    pack[me_p, 0:nb, 0:ple] = raw_t / jnp.sum(raw_t, axis=0, keepdims=True)
    pack[me_p, nb : nb + 1, 0:ple] = amp[...]
    pack[me_p, 0:nb, ple : 2 * ple] = jnp.transpose(offs[...].astype(F32))

    v_pad[...] = jnp.zeros(v_pad.shape, F32)
    v_pad[:, 0:length] = vec[me_s]
    loads[0].wait()
    source = dot3(v_pad[...], fwd[0], fwd[1])
    for index in range(n_pts):
        a_send[index] = source[:, index * cfp : (index + 1) * cfp]

    pl.semaphore_wait(barrier, n_pts - 1 + n_sens - 1)
    pack_args = (lambda _: pack.at[me_p], lambda i: pack.at[i], pack_s, pack_r)
    send_pts(*pack_args)
    a_args = (lambda i: a_send.at[i], lambda i: a_recv.at[i], a_s, a_r)
    send_pts(*a_args)
    a_recv[me_p] = a_send[me_p]

    loads[1].wait()
    loads[2].wait()

    def halve(index, carry):
        for part in range(2):
            high, low = split(k_f32[part, index])
            k_hl[index, part * sl : (part + 1) * sl] = high
            k_hl[index, (2 + part) * sl : (3 + part) * sl] = low
        return carry

    lax.fori_loop(0, fb, halve, 0)
    for index in range(fb, fbp):
        k_hl[index] = jnp.zeros(k_hl.shape[1:], BF)

    for step in pts_steps:
        arrive_pts(step, *pack_args)
    gathered = [pack[index] for index in range(n_pts)]
    weights_row = jnp.concatenate([block[:, 0:ple] for block in gathered], axis=1)
    offsets_row = jnp.concatenate([block[:, ple : 2 * ple] for block in gathered], axis=1)
    down = lax.broadcasted_iota(jnp.int32, (pt, pt), 0)
    across = lax.broadcasted_iota(jnp.int32, (pt, pt), 1)
    shift = (down - across).astype(F32)
    mean_t = jnp.zeros((pt, pt), F32)
    for k in range(nb):
        mean_t = mean_t + jnp.where(
            shift == offsets_row[k : k + 1], weights_row[k : k + 1], 0.0
        )
    identity = jnp.where(down == across, 1.0, 0.0).astype(F32)
    before, now = identity, mean_t
    total = cheb[0] * before + cheb[1] * now
    mean_h, mean_l = split(mean_t)
    for degree in range(2, cheb.shape[0]):
        before, now = now, 2.0 * dot3(now, mean_h, mean_l) - before
        total = total + cheb[degree] * now
    prior_t = total * weights_row[nb : nb + 1]
    prior_h, prior_l = split(prior_t)

    for step in pts_steps:
        arrive_pts(step, *a_args)
    by_point = a_recv[...].reshape(pt, cfp)
    own = dot3(jnp.transpose(by_point), prior_h, prior_l)
    tiles = pt // 128
    for part in range(2):
        for tile in range(tiles):
            spec[part, me_s, tile] = own[
                part * fbp : (part + 1) * fbp, tile * 128 : (tile + 1) * 128
            ]
    s_args = (lambda _: spec.at[:, me_s], lambda i: spec.at[:, i], s_s, s_r)
    send_sens(*s_args)
    for step in sens_steps:
        arrive_sens(step, *s_args)

    spec_rows = spec.reshape(rows * tiles * fbp, 128)

    def predict(index, carry):
        values = jnp.concatenate(
            [
                spec_rows[pl.ds(tile * fbp + index, rows, stride=tiles * fbp), :]
                for tile in range(tiles)
            ],
            axis=1,
        )
        high, low = split(values)
        product = lax.dot_general(
            jnp.concatenate([high, low], axis=0), k_hl[index], NT, preferred_element_type=F32
        )
        y_buf[index] = (
            product[:rows, : 2 * sl] + product[rows:, : 2 * sl] + product[:rows, 2 * sl :]
        )
        return carry

    lax.fori_loop(0, fbp, predict, 0, unroll=8)

    y_rows = y_buf.reshape(fbp * rows, 2 * sl)
    blank = jnp.zeros((cfp - 2 * fbp, 2 * sl), F32)
    for v in range(nv):
        real = y_rows[pl.ds(v, fbp, stride=rows), :]
        imag = y_rows[pl.ds(nv + v, fbp, stride=rows), :]
        direct = jnp.concatenate([real, imag, blank], axis=0)
        crossed = jnp.concatenate([-imag, real, blank], axis=0)
        data = jnp.transpose(direct + pltpu.roll(crossed, sl, 1))
        for index in range(n_pts):
            d_send[index, v] = data[index * sq : (index + 1) * sq]
    d_args = (lambda i: d_send.at[i], lambda i: d_recv.at[i], d_s, d_r)
    send_pts(*d_args)
    d_recv[me_p] = d_send[me_p]
    loads[3].wait()
    which = lax.rem(lax.broadcasted_iota(jnp.int32, (nv * sq, 1), 0), sq)
    precision = jnp.zeros((nv * sq, 1), F32)
    for index in range(sq):
        precision = jnp.where(which == index, noise[index], precision)
    for step in pts_steps:
        arrive_pts(step, *d_args)
    data_spec = jnp.concatenate(
        [d_recv[index].reshape(nv * sq, cfp) for index in range(n_pts)], axis=1
    )
    data = dot3(data_spec, inv[0], inv[1]) * precision
    back = dot3(data, fwd[0], fwd[1])
    for index in range(n_pts):
        e_send[index] = back[:, index * cfp : (index + 1) * cfp].reshape(nv, sq, cfp)
    e_args = (lambda i: e_send.at[i], lambda i: e_recv.at[i], e_s, e_r)
    send_pts(*e_args)
    e_recv[me_p] = e_send[me_p]
    for step in pts_steps:
        arrive_pts(step, *e_args)
    for v in range(nv):
        turned = jnp.transpose(
            jnp.concatenate([e_recv[index, v] for index in range(n_pts)], axis=0)
        )
        real, imag = turned[:fbp], turned[fbp : 2 * fbp]
        l_buf[0, v] = jnp.concatenate([real, imag], axis=1)
        l_buf[1, v] = jnp.concatenate([imag, -real], axis=1)

    l_rows = l_buf.reshape(rows * fbp, 2 * sl)
    g_rows = g_buf.reshape(rows * tiles * fbp, 128)

    def adjoint(index, carry):
        values = l_rows[pl.ds(index, rows, stride=fbp), :]
        high, low = split(values)
        left = jnp.concatenate(
            [
                jnp.concatenate([high, high], axis=1),
                jnp.concatenate([low, jnp.zeros_like(low)], axis=1),
            ],
            axis=0,
        )
        product = lax.dot_general(left, k_hl[index], NN, preferred_element_type=F32)
        result = product[:rows] + product[rows:]
        for tile in range(tiles):
            g_rows[pl.ds(tile * fbp + index, rows, stride=tiles * fbp), :] = result[
                :, tile * 128 : (tile + 1) * 128
            ]
        return carry

    lax.fori_loop(0, fbp, adjoint, 0, unroll=8)

    g_args = (lambda i: g_buf.at[:, i], lambda i: r_recv.at[i], g_s, g_r)
    send_sens(*g_args)
    gradient = g_buf[:, me_s]
    for step in sens_steps:
        arrive_sens(step, *g_args)
        gradient = gradient + r_recv[lax.rem(me_s - step + n_sens, n_sens)]
    gradient = jnp.concatenate(
        [
            jnp.concatenate([gradient[part, tile] for tile in range(tiles)], axis=1)
            for part in range(2)
        ]
        + [jnp.zeros((cfp - 2 * fbp, pt), F32)],
        axis=0,
    )
    grad_h, grad_l = split(gradient)
    h_send[...] = dot3(prior_t, grad_h, grad_l, NT).reshape(h_send.shape)
    h_args = (lambda i: h_send.at[i], lambda i: h_recv.at[i], h_s, h_r)
    send_pts(*h_args)
    h_recv[me_p] = h_send[me_p]
    for step in pts_steps:
        arrive_pts(step, *h_args)
    last = jnp.concatenate([h_recv[index] for index in range(n_pts)], axis=1)
    o_buf[me_s] = dot3(last, inv[0], inv[1])
    o_args = (lambda _: o_buf.at[me_s], lambda i: o_buf.at[i], o_s, o_r)
    send_sens(*o_args)
    out[me_s] = vec[me_s] + o_buf[me_s, :, 0:length]
    for step in sens_steps:
        arrive_sens(step, *o_args)
        other = lax.rem(me_s - step + n_sens, n_sens)
        out[other] = vec[other] + o_buf[other, :, 0:length]
    for copy in started:
        copy.wait_send()


def local(vectors, kernel_hat, noise_prec, stencil_coefficients_raw, offsets, amplitude, cheb_coef):
    n_sens, n_pts = lax.axis_size("sens"), lax.axis_size("pts")
    nv, ple, length = vectors.shape
    fb, sl, pt = kernel_hat.shape[1:]
    nb = offsets.shape[1]
    fbp = up(fb, 8)
    cfp = up(2 * fbp, 128)
    tp = up(length, 128)
    sq = sl // n_pts
    fits = (
        nv == n_sens
        and 2 * nv == 8
        and nb < 8
        and ple % 8 == 0
        and 2 * ple <= 128
        and sl == sq * n_pts
        and sq % 8 == 0
        and 2 * sl == 128
        and pt % 128 == 0
        and kernel_hat.size < 2**21
    )
    if not fits:
        return plain(
            vectors, kernel_hat, noise_prec, stencil_coefficients_raw, offsets, amplitude, cheb_coef
        )
    forward, inverse = host_tables(length, fb, n_pts, fbp, cfp, tp)
    sizes = (nv, n_sens, n_pts, fb, fbp, cfp, sl, sq, pt, ple, length, tp)
    vmem = pl.BlockSpec(memory_space=pltpu.VMEM)
    smem = pl.BlockSpec(memory_space=pltpu.SMEM)
    anywhere = pl.BlockSpec(memory_space=pl.ANY)
    wide = n_pts * cfp

    def f32(*shape):
        return pltpu.VMEM(shape, F32)

    def sems(count):
        return pltpu.SemaphoreType.DMA((count,))

    return pl.pallas_call(
        functools.partial(fused_kernel, sizes),
        out_shape=jax.ShapeDtypeStruct(vectors.shape, F32),
        in_specs=[vmem, anywhere, smem, vmem, vmem, vmem, smem, anywhere, anywhere],
        out_specs=vmem,
        scratch_shapes=[
            pltpu.VMEM((2, tp, wide), BF),
            pltpu.VMEM((2, wide, tp), BF),
            f32(2, fb, sl, pt),
            pltpu.VMEM((fbp, 4 * sl, pt), BF),
            f32(ple, tp),
            f32(n_pts, 8, 128),
            f32(n_pts, ple, cfp),
            f32(n_pts, ple, cfp),
            f32(2, nv, pt // 128, fbp, 128),
            f32(fbp, 2 * nv, 2 * sl),
            f32(n_pts, nv, sq, cfp),
            f32(n_pts, nv, sq, cfp),
            f32(n_pts, nv, sq, cfp),
            f32(n_pts, nv, sq, cfp),
            f32(2, nv, fbp, 2 * sl),
            f32(2, nv, pt // 128, fbp, 128),
            f32(n_sens, 2, pt // 128, fbp, 128),
            f32(n_pts, ple, cfp),
            f32(n_pts, ple, cfp),
            f32(nv, ple, tp),
            sems(4),
            *[sems(n_pts)] * 4,
            *[sems(n_sens)] * 2,
            *[sems(n_pts)] * 4,
            *[sems(n_sens)] * 2,
            *[sems(n_pts)] * 2,
            *[sems(n_sens)] * 2,
        ],
        compiler_params=pltpu.CompilerParams(
            collective_id=0, has_side_effects=True, vmem_limit_bytes=56 * 2**20
        ),
    )(
        vectors, kernel_hat, noise_prec, stencil_coefficients_raw, offsets,
        amplitude.reshape(1, ple), cheb_coef, forward, inverse,
    )


def solution(mesh):
    placed = (
        P(None, "pts", None),
        P(None, "pts", "sens", None),
        P(("sens", "pts")),
        P("pts", None),
        P("pts", None),
        P("pts"),
        P(),
    )
    return jax.shard_map(
        local, mesh=mesh, in_specs=placed, out_specs=P(None, "pts", None), check_vma=False
    )
```

```python
import functools

import jax
import jax.numpy as jnp
import ml_dtypes
import numpy as np
from jax import lax
from jax.experimental import pallas as pl
from jax.experimental.pallas import tpu as pltpu
from jax.sharding import PartitionSpec as P

exact_evaluation_flag = lax.Precision.HIGHEST


def transform_tables(length, padded):
    time_index = jnp.arange(length, dtype=jnp.int32)
    frequency = jnp.arange(padded, dtype=jnp.int32)
    period = 2 * length
    phase_index = frequency[:, None] * time_index[None, :] % period
    angles = 2.0 * jnp.pi / period * phase_index.astype(jnp.float32)
    active = (frequency <= length).astype(jnp.float32)[:, None]
    cosine = jnp.cos(angles)
    sine_part = jnp.sin(angles)
    forward_operator = jnp.stack([cosine * active, -sine_part * active])
    edge_rows = (frequency == 0) | (frequency == length)
    weight = jnp.where(edge_rows, 1.0, 2.0).astype(jnp.float32)[:, None] * active / period
    inverse = jnp.stack([cosine * weight, -sine_part * weight])
    return (forward_operator, inverse)


def to_spectrum(time_series_values, forward_operator):
    return jnp.einsum(
        "vpt,cft->vcfp", time_series_values, forward_operator, precision=exact_evaluation_flag
    )


def to_series(spectrum, inverse):
    return jnp.einsum("vcfp,cft->vpt", spectrum, inverse, precision=exact_evaluation_flag)


def chebyshev(values_in, operator, cheb_coef):
    previous = values_in
    current = operator(values_in)
    running_sum = cheb_coef[0] * previous + cheb_coef[1] * current
    for degree in range(2, cheb_coef.shape[0]):
        following = 2.0 * operator(current) - previous
        previous, current = (current, following)
        running_sum = running_sum + cheb_coef[degree] * current
    return running_sum


def full_matrix(weights_all, offsets_all):
    point_count = weights_all.shape[0]
    positions = jnp.arange(point_count, dtype=jnp.int32)
    target = positions[:, None] + offsets_all
    dense_operator_matrix = jnp.zeros((point_count, point_count), jnp.float32)
    for column in range(weights_all.shape[1]):
        hit = (target[:, column][:, None] == positions[None, :]).astype(jnp.float32)
        dense_operator_matrix = dense_operator_matrix + weights_all[:, column][:, None] * hit
    return dense_operator_matrix


def plain(vectors, kernel_hat, noise_prec, stencil_coefficients_raw, offsets, amplitude, cheb_coef):
    length = vectors.shape[2]
    freq_block = kernel_hat.shape[1]
    padded = freq_block * lax.axis_size("pts")
    forward_operator, inverse = transform_tables(length, padded)
    weights = stencil_coefficients_raw / jnp.sum(stencil_coefficients_raw, axis=1, keepdims=True)
    kernel_real = kernel_hat[0]
    kernel_imag = kernel_hat[1]
    offsets_all = lax.all_gather(offsets, "pts", axis=0, tiled=True)
    weights_all, amplitude_all = (
        lax.all_gather(weights, "pts", axis=0, tiled=True),
        lax.all_gather(amplitude, "pts", axis=0, tiled=True),
    )
    dense_operator_matrix = full_matrix(weights_all, offsets_all)

    def forward_mean(values):
        return jnp.einsum(
            "vcfq,pq->vcfp", values, dense_operator_matrix, precision=exact_evaluation_flag
        )

    def backward_mean(values):
        return jnp.einsum(
            "vcfp,pq->vcfq", values, dense_operator_matrix, precision=exact_evaluation_flag
        )

    source = to_spectrum(vectors, forward_operator)
    spectrum = lax.all_to_all(source, "pts", split_axis=2, concat_axis=3, tiled=True)
    spectrum = amplitude_all[None, None, None, :] * chebyshev(spectrum, forward_mean, cheb_coef)
    real_part = spectrum[:, 0]
    imag_part = spectrum[:, 1]
    data_real = jnp.einsum(
        "fsp,vfp->vfs", kernel_real, real_part, precision=exact_evaluation_flag
    ) - jnp.einsum("fsp,vfp->vfs", kernel_imag, imag_part, precision=exact_evaluation_flag)
    data_imag = jnp.einsum(
        "fsp,vfp->vfs", kernel_real, imag_part, precision=exact_evaluation_flag
    ) + jnp.einsum("fsp,vfp->vfs", kernel_imag, real_part, precision=exact_evaluation_flag)
    data_spec = jnp.stack([data_real, data_imag], axis=1)
    time_series_values = (
        jnp.einsum(
            "rklu,klq->ruq",
            lax.all_to_all(data_spec, "pts", split_axis=3, concat_axis=2, tiled=True),
            inverse,
            precision=exact_evaluation_flag,
        )
        * noise_prec[None, :, None]
    )
    weighted_result = jnp.einsum(
        "lew,jkw->ljke", time_series_values, forward_operator, precision=exact_evaluation_flag
    )
    weighted_result = lax.all_to_all(
        weighted_result, "pts", split_axis=2, concat_axis=3, tiled=True
    )
    back_real = weighted_result[:, 0]
    back_imag = weighted_result[:, 1]
    grad_real = jnp.einsum(
        "fsp,vfs->vfp", kernel_real, back_real, precision=exact_evaluation_flag
    ) + jnp.einsum("fsp,vfs->vfp", kernel_imag, back_imag, precision=exact_evaluation_flag)
    grad_imag = jnp.einsum(
        "fsp,vfs->vfp", kernel_real, back_imag, precision=exact_evaluation_flag
    ) - jnp.einsum("fsp,vfs->vfp", kernel_imag, back_real, precision=exact_evaluation_flag)
    partial_value = chebyshev(
        amplitude_all[None, None, None, :] * jnp.stack([grad_real, grad_imag], axis=1),
        backward_mean,
        cheb_coef,
    )
    summed = lax.psum(partial_value, "sens")
    moved = lax.all_to_all(summed, "pts", split_axis=3, concat_axis=2, tiled=True)
    gradient = to_series(moved, inverse)
    return vectors + gradient


BF = jnp.bfloat16
F32 = jnp.float32
MESH = pl.DeviceIdType.MESH


def up(size, multiple):
    return -(-size // multiple) * multiple


def host_tables(length, block, blocks, padded_block, lanes, padded_time):
    period = 2 * length
    forward = np.zeros((padded_time, blocks, lanes))
    inverse = np.zeros((blocks, lanes, padded_time))
    time = np.arange(length)
    for index in range(blocks):
        frequency = index * block + np.arange(block)
        angle = 2.0 * np.pi / period * (frequency[:, None] * time[None, :] % period)
        active = (frequency <= length)[:, None]
        edge = (frequency == 0) | (frequency == length)
        weight = np.where(edge, 1.0, 2.0)[:, None] / period
        for part, table in enumerate((np.cos(angle) * active, -np.sin(angle) * active)):
            at = slice(part * padded_block, part * padded_block + block)
            forward[:length, index, at] = table.T
            inverse[index, at, :length] = table * weight
    forward = forward.reshape(padded_time, blocks // 2, 2 * lanes).transpose(1, 0, 2)
    inverse = inverse.reshape(blocks // 2, 2 * lanes, padded_time)
    halves = []
    for table in (forward, inverse):
        high = table.astype(ml_dtypes.bfloat16)
        low = (table - high.astype(np.float64)).astype(ml_dtypes.bfloat16)
        halves.append(np.stack([high, low]))
    return halves


def split(values):
    high = values.astype(BF)
    return high, (values - high.astype(F32)).astype(BF)


NN = (((1,), (0,)), ((), ()))
NT = (((1,), (1,)), ((), ()))


def dot3(left, right_high, right_low, dims=NN):
    rows = left.shape[0]
    high, low = split(left)
    both = lax.dot_general(
        jnp.concatenate([high, low], axis=0), right_high, dims, preferred_element_type=F32
    )
    cross = lax.dot_general(high, right_low, dims, preferred_element_type=F32)
    return both[:rows] + both[rows:] + cross


def flip(index, step, size):
    flipped, bit = 0, 1
    while bit < size:
        digit = lax.rem(index // bit, 2)
        flipped = flipped + bit * ((1 - digit) if step & bit else digit)
        bit *= 2
    return flipped


def fused_kernel(
    sizes,
    vec, kern, noise, raw, offs, amp, cheb, fwd_in, inv_in,
    out,
    fwd, inv, k_f32, k_hl, v_own, v_pad, pack, a_send, x_all, spec, y_buf, d_send, d_recv,
    e_send, e_recv, l_buf, g_buf, r_recv, h_send, h_recv, o_buf,
    load_sem, pack_s, pack_r, a_s, a_r, f_s, f_r, d_s, d_r, e_s, e_r, g_s, g_r, h_s, h_r, o_s, o_r,
):
    nv, n_sens, n_pts, fb, fbp, cfp, sl, sq, pt, ple, length, tp = sizes
    me_s = lax.axis_index("sens")
    me_p = lax.axis_index("pts")
    rows = 2 * nv
    tiles = pt // 128
    pairs = n_pts // 2
    my_pair = me_p // 2
    pts_steps = range(1, n_pts)
    sens_steps = range(1, n_sens)
    pts_peer = [flip(me_p, step, n_pts) for step in range(n_pts)]
    sens_peer = [flip(me_s, step, n_sens) for step in range(n_sens)]
    pair_peer = [flip(my_pair, step, pairs) for step in range(pairs)]

    loads = [
        pltpu.make_async_copy(vec.at[me_s], v_own, load_sem.at[0]),
        pltpu.make_async_copy(fwd_in, fwd, load_sem.at[1]),
        pltpu.make_async_copy(kern.at[0], k_f32.at[0], load_sem.at[2]),
        pltpu.make_async_copy(kern.at[1], k_f32.at[1], load_sem.at[3]),
        pltpu.make_async_copy(inv_in, inv, load_sem.at[4]),
    ]
    loads[0].start()
    loads[1].start()

    barrier = pltpu.get_barrier_semaphore()
    for step in pts_steps:
        pl.semaphore_signal(
            barrier, inc=1, device_id=(me_s, pts_peer[step]), device_id_type=MESH
        )
    for step in sens_steps:
        pl.semaphore_signal(
            barrier, inc=1, device_id=(sens_peer[step], me_p), device_id_type=MESH
        )

    started = []

    def copy_pts(step, src, dst, send_sem, recv_sem):
        return pltpu.make_async_remote_copy(
            src_ref=src, dst_ref=dst, send_sem=send_sem.at[step], recv_sem=recv_sem.at[step],
            device_id=(me_s, pts_peer[step]), device_id_type=MESH,
        )

    def copy_sens(step, slot, src, dst, send_sem, recv_sem):
        at = slot * n_sens + step
        return pltpu.make_async_remote_copy(
            src_ref=src, dst_ref=dst, send_sem=send_sem.at[at], recv_sem=recv_sem.at[at],
            device_id=(sens_peer[step], me_p), device_id_type=MESH,
        )

    def go(copy):
        copy.start()
        started.append(copy)

    nb = raw.shape[0]
    pack[me_p] = jnp.zeros(pack.shape[1:], F32)
    raw_t = raw[...]
    pack[me_p, 0:nb, 0:ple] = raw_t / jnp.sum(raw_t, axis=0, keepdims=True)
    pack[me_p, nb : nb + 1, 0:ple] = amp[...]
    pack[me_p, 0:nb, ple : 2 * ple] = offs[...].astype(F32)

    v_pad[...] = jnp.zeros(v_pad.shape, F32)
    loads[0].wait()
    v_pad[:, 0:length] = v_own[...]
    loads[1].wait()
    for load in loads[2:]:
        load.start()
    pl.semaphore_wait(barrier, n_pts - 1 + n_sens - 1)

    for step in pts_steps:
        go(copy_pts(step, pack.at[me_p], pack.at[me_p], pack_s, pack_r))

    high, low = split(v_pad[...])
    both = jnp.concatenate([high, low], axis=0)
    for turn in list(range(1, pairs)) + [0]:
        pair = pair_peer[turn]
        part = jnp.dot(both, fwd[0, pair], preferred_element_type=F32)
        source = part[:ple] + part[ple:] + jnp.dot(high, fwd[1, pair], preferred_element_type=F32)
        for side in range(2):
            a_send[2 * pair + side] = source[:, side * cfp : (side + 1) * cfp]
        for step in (2 * turn, 2 * turn + 1):
            if step:
                go(copy_pts(step, a_send.at[pts_peer[step]], x_all.at[me_s, me_p], a_s, a_r))
    x_all[me_s, me_p] = a_send[me_p]

    def hand_on(step):
        for other in sens_steps:
            block = x_all.at[me_s, pts_peer[step]]
            go(copy_sens(other, step, block, block, f_s, f_r))

    hand_on(0)

    loads[2].wait()
    loads[3].wait()

    def halve(index, carry):
        for part in range(2):
            high, low = split(k_f32[part, index])
            k_hl[index, part * sl : (part + 1) * sl] = high
            k_hl[index, (2 + part) * sl : (3 + part) * sl] = low
        return carry

    share = -(-fb // (n_pts - 1))
    for step in pts_steps:
        lax.fori_loop(min((step - 1) * share, fb), min(step * share, fb), halve, 0, unroll=2)
        block = x_all.at[me_s, pts_peer[step]]
        copy_pts(step, block, block, a_s, a_r).wait_recv()
        hand_on(step)
    for index in range(fb, fbp):
        k_hl[index] = jnp.zeros(k_hl.shape[1:], BF)

    for step in pts_steps:
        block = pack.at[pts_peer[step]]
        copy_pts(step, block, block, pack_s, pack_r).wait_recv()
    gathered = [pack[index] for index in range(n_pts)]
    weights_row = jnp.concatenate([block[:, 0:ple] for block in gathered], axis=1)
    offsets_row = jnp.concatenate([block[:, ple : 2 * ple] for block in gathered], axis=1)
    down = lax.broadcasted_iota(jnp.int32, (pt, pt), 0)
    across = lax.broadcasted_iota(jnp.int32, (pt, pt), 1)
    shift = (down - across).astype(F32)
    mean_t = jnp.zeros((pt, pt), F32)
    for k in range(nb):
        mean_t = mean_t + jnp.where(
            shift == offsets_row[k : k + 1], weights_row[k : k + 1], 0.0
        )
    identity = jnp.where(down == across, 1.0, 0.0).astype(F32)
    before, now = identity, mean_t
    total = cheb[0] * before + cheb[1] * now
    mean_h, mean_l = split(mean_t)
    for degree in range(2, cheb.shape[0]):
        before, now = now, 2.0 * dot3(now, mean_h, mean_l) - before
        total = total + cheb[degree] * now
    prior_t = total * weights_row[nb : nb + 1]
    prior_h, prior_l = split(prior_t)

    for other in range(n_sens):
        v = sens_peer[other]
        if other:
            for step in range(n_pts):
                block = x_all.at[v, pts_peer[step]]
                copy_sens(other, step, block, block, f_s, f_r).wait_recv()
        own = dot3(jnp.transpose(x_all[v].reshape(pt, cfp)), prior_h, prior_l)
        for part in range(2):
            for tile in range(tiles):
                spec[part, v, tile] = own[
                    part * fbp : (part + 1) * fbp, tile * 128 : (tile + 1) * 128
                ]

    spec_rows = spec.reshape(rows * tiles * fbp, 128)

    def predict(index, carry):
        values = jnp.concatenate(
            [
                spec_rows[pl.ds(tile * fbp + index, rows, stride=tiles * fbp), :]
                for tile in range(tiles)
            ],
            axis=1,
        )
        high, low = split(values)
        product = lax.dot_general(
            jnp.concatenate([high, low], axis=0), k_hl[index], NT, preferred_element_type=F32
        )
        y_buf[index] = (
            product[:rows, : 2 * sl] + product[rows:, : 2 * sl] + product[:rows, 2 * sl :]
        )
        return carry

    lax.fori_loop(0, fbp, predict, 0, unroll=8)

    y_rows = y_buf.reshape(fbp * rows, 2 * sl)
    blank = jnp.zeros((cfp - 2 * fbp, 2 * sl), F32)
    for v in range(nv):
        real = y_rows[pl.ds(v, fbp, stride=rows), :]
        imag = y_rows[pl.ds(nv + v, fbp, stride=rows), :]
        direct = jnp.concatenate([real, imag, blank], axis=0)
        crossed = jnp.concatenate([-imag, real, blank], axis=0)
        data = jnp.transpose(direct + pltpu.roll(crossed, sl, 1))
        for index in range(n_pts):
            d_send[index, v] = data[index * sq : (index + 1) * sq]
    for step in reversed(pts_steps):
        go(copy_pts(step, d_send.at[pts_peer[step]], d_recv.at[me_p], d_s, d_r))
    d_recv[me_p] = d_send[me_p]
    loads[4].wait()
    which = lax.rem(lax.broadcasted_iota(jnp.int32, (nv * sq, 1), 0), sq)
    precision = jnp.zeros((nv * sq, 1), F32)
    for index in range(sq):
        precision = jnp.where(which == index, noise[index], precision)

    def series(received, lines, send_sem, recv_sem):
        result = jnp.zeros((lines, tp), F32)
        for turn in range(pairs):
            for step in (2 * turn, 2 * turn + 1):
                if step:
                    block = received.at[pts_peer[step]]
                    copy_pts(step, block, block, send_sem, recv_sem).wait_recv()
            pair = pair_peer[turn]
            both = jnp.concatenate(
                [received[2 * pair + side].reshape(lines, cfp) for side in range(2)], axis=1
            )
            result = result + dot3(both, inv[0, pair], inv[1, pair])
        return result

    data = series(d_recv, nv * sq, d_s, d_r) * precision
    high, low = split(data)
    both = jnp.concatenate([high, low], axis=0)
    lines = nv * sq
    for turn in list(range(1, pairs)) + [0]:
        pair = pair_peer[turn]
        part = jnp.dot(both, fwd[0, pair], preferred_element_type=F32)
        back = part[:lines] + part[lines:] + jnp.dot(high, fwd[1, pair], preferred_element_type=F32)
        for side in range(2):
            e_send[2 * pair + side] = back[:, side * cfp : (side + 1) * cfp].reshape(nv, sq, cfp)
        for step in (2 * turn, 2 * turn + 1):
            if step:
                go(copy_pts(step, e_send.at[pts_peer[step]], e_recv.at[me_p], e_s, e_r))
    e_recv[me_p] = e_send[me_p]
    for step in pts_steps:
        block = e_recv.at[pts_peer[step]]
        copy_pts(step, block, block, e_s, e_r).wait_recv()
    for v in range(nv):
        turned = jnp.transpose(
            jnp.concatenate([e_recv[index, v] for index in range(n_pts)], axis=0)
        )
        real, imag = turned[:fbp], turned[fbp : 2 * fbp]
        l_buf[0, v] = jnp.concatenate([real, imag], axis=1)
        l_buf[1, v] = jnp.concatenate([imag, -real], axis=1)

    l_rows = l_buf.reshape(rows * fbp, 2 * sl)
    g_rows = g_buf.reshape(rows * tiles * fbp, 128)

    def adjoint(index, carry):
        values = l_rows[pl.ds(index, rows, stride=fbp), :]
        high, low = split(values)
        left = jnp.concatenate(
            [
                jnp.concatenate([high, high], axis=1),
                jnp.concatenate([low, jnp.zeros_like(low)], axis=1),
            ],
            axis=0,
        )
        product = lax.dot_general(left, k_hl[index], NN, preferred_element_type=F32)
        result = product[:rows] + product[rows:]
        for tile in range(tiles):
            g_rows[pl.ds(tile * fbp + index, rows, stride=tiles * fbp), :] = result[
                :, tile * 128 : (tile + 1) * 128
            ]
        return carry

    groups = [(at, min(16, fbp - at)) for at in range(0, fbp, 16)]
    for slot, (at, count) in enumerate(groups):
        lax.fori_loop(at, at + count, adjoint, 0, unroll=8)
        for step in reversed(sens_steps):
            go(
                copy_sens(
                    step, slot,
                    g_buf.at[:, sens_peer[step], :, pl.ds(at, count), :],
                    r_recv.at[me_s, :, :, pl.ds(at, count), :],
                    g_s, g_r,
                )
            )
    gradient = g_buf[:, me_s]
    for slot, (at, count) in enumerate(groups):
        for step in sens_steps:
            block = r_recv.at[sens_peer[step], :, :, pl.ds(at, count), :]
            copy_sens(step, slot, block, block, g_s, g_r).wait_recv()
    for step in sens_steps:
        gradient = gradient + r_recv[sens_peer[step]]
    gradient = jnp.concatenate(
        [
            jnp.concatenate([gradient[part, tile] for tile in range(tiles)], axis=1)
            for part in range(2)
        ]
        + [jnp.zeros((cfp - 2 * fbp, pt), F32)],
        axis=0,
    )
    grad_h, grad_l = split(gradient)
    h_send[...] = dot3(prior_t, grad_h, grad_l, NT).reshape(h_send.shape)
    for step in reversed(pts_steps):
        go(copy_pts(step, h_send.at[pts_peer[step]], h_recv.at[me_p], h_s, h_r))
    h_recv[me_p] = h_send[me_p]
    o_buf[me_s] = series(h_recv, ple, h_s, h_r)
    for step in reversed(sens_steps):
        go(copy_sens(step, 0, o_buf.at[me_s], o_buf.at[me_s], o_s, o_r))
    out[me_s] = o_buf[me_s, :, 0:length]
    for step in sens_steps:
        block = o_buf.at[sens_peer[step]]
        copy_sens(step, 0, block, block, o_s, o_r).wait_recv()
        out[sens_peer[step]] = o_buf[sens_peer[step], :, 0:length]
    for copy in started:
        copy.wait_send()


def local(vectors, kernel_hat, noise_prec, stencil_coefficients_raw, offsets, amplitude, cheb_coef):
    n_sens, n_pts = lax.axis_size("sens"), lax.axis_size("pts")
    nv, ple, length = vectors.shape
    fb, sl, pt = kernel_hat.shape[1:]
    nb = offsets.shape[1]
    fbp = up(fb, 8)
    cfp = up(2 * fbp, 128)
    tp = up(length, 128)
    sq = sl // n_pts
    fits = (
        nv == n_sens
        and 2 * nv == 8
        and n_pts & (n_pts - 1) == 0
        and n_pts > 1
        and nb < 8
        and ple % 8 == 0
        and 2 * ple <= 128
        and sl == sq * n_pts
        and sq % 8 == 0
        and 2 * sl == 128
        and pt % 128 == 0
        and kernel_hat.size < 2**21
    )
    if not fits:
        return plain(
            vectors, kernel_hat, noise_prec, stencil_coefficients_raw, offsets, amplitude, cheb_coef
        )
    forward, inverse = host_tables(length, fb, n_pts, fbp, cfp, tp)
    sizes = (nv, n_sens, n_pts, fb, fbp, cfp, sl, sq, pt, ple, length, tp)
    vmem = pl.BlockSpec(memory_space=pltpu.VMEM)
    smem = pl.BlockSpec(memory_space=pltpu.SMEM)
    anywhere = pl.BlockSpec(memory_space=pl.ANY)

    def f32(*shape):
        return pltpu.VMEM(shape, F32)

    def sems(count):
        return pltpu.SemaphoreType.DMA((count,))

    gradient = pl.pallas_call(
        functools.partial(fused_kernel, sizes),
        out_shape=jax.ShapeDtypeStruct(vectors.shape, F32),
        in_specs=[anywhere, anywhere, smem, vmem, vmem, vmem, smem, anywhere, anywhere],
        out_specs=vmem,
        scratch_shapes=[
            pltpu.VMEM(forward.shape, BF),
            pltpu.VMEM(inverse.shape, BF),
            f32(2, fb, sl, pt),
            pltpu.VMEM((fbp, 4 * sl, pt), BF),
            f32(ple, length),
            f32(ple, tp),
            f32(n_pts, 8, 128),
            f32(n_pts, ple, cfp),
            f32(nv, n_pts, ple, cfp),
            f32(2, nv, pt // 128, fbp, 128),
            f32(fbp, 2 * nv, 2 * sl),
            f32(n_pts, nv, sq, cfp),
            f32(n_pts, nv, sq, cfp),
            f32(n_pts, nv, sq, cfp),
            f32(n_pts, nv, sq, cfp),
            f32(2, nv, fbp, 2 * sl),
            f32(2, nv, pt // 128, fbp, 128),
            f32(n_sens, 2, pt // 128, fbp, 128),
            f32(n_pts, ple, cfp),
            f32(n_pts, ple, cfp),
            f32(nv, ple, tp),
            sems(5),
            *[sems(n_pts)] * 4,
            *[sems(n_pts * n_sens)] * 2,
            *[sems(n_pts)] * 4,
            *[sems(up(fbp, 16) // 16 * n_sens)] * 2,
            *[sems(n_pts)] * 2,
            *[sems(n_sens)] * 2,
        ],
        compiler_params=pltpu.CompilerParams(
            collective_id=0, has_side_effects=True, vmem_limit_bytes=56 * 2**20
        ),
    )(
        vectors, kernel_hat, noise_prec, stencil_coefficients_raw.T, offsets.T,
        amplitude.reshape(1, ple), cheb_coef, forward, inverse,
    )
    return vectors + gradient


def solution(mesh):
    placed = (
        P(None, "pts", None),
        P(None, "pts", "sens", None),
        P(("sens", "pts")),
        P("pts", None),
        P("pts", None),
        P("pts"),
        P(),
    )
    return jax.shard_map(
        local, mesh=mesh, in_specs=placed, out_specs=P(None, "pts", None), check_vma=False
    )
```

```python
import functools

import jax
import jax.numpy as jnp
import ml_dtypes
import numpy as np
from jax import lax
from jax.experimental import pallas as pl
from jax.experimental.pallas import tpu as pltpu
from jax.sharding import PartitionSpec as P

exact_evaluation_flag = lax.Precision.HIGHEST


def transform_tables(length, padded):
    time_index = jnp.arange(length, dtype=jnp.int32)
    frequency = jnp.arange(padded, dtype=jnp.int32)
    period = 2 * length
    phase_index = frequency[:, None] * time_index[None, :] % period
    angles = 2.0 * jnp.pi / period * phase_index.astype(jnp.float32)
    active = (frequency <= length).astype(jnp.float32)[:, None]
    cosine = jnp.cos(angles)
    sine_part = jnp.sin(angles)
    forward_operator = jnp.stack([cosine * active, -sine_part * active])
    edge_rows = (frequency == 0) | (frequency == length)
    weight = jnp.where(edge_rows, 1.0, 2.0).astype(jnp.float32)[:, None] * active / period
    inverse = jnp.stack([cosine * weight, -sine_part * weight])
    return (forward_operator, inverse)


def to_spectrum(time_series_values, forward_operator):
    return jnp.einsum(
        "vpt,cft->vcfp", time_series_values, forward_operator, precision=exact_evaluation_flag
    )


def to_series(spectrum, inverse):
    return jnp.einsum("vcfp,cft->vpt", spectrum, inverse, precision=exact_evaluation_flag)


def chebyshev(values_in, operator, cheb_coef):
    previous = values_in
    current = operator(values_in)
    running_sum = cheb_coef[0] * previous + cheb_coef[1] * current
    for degree in range(2, cheb_coef.shape[0]):
        following = 2.0 * operator(current) - previous
        previous, current = (current, following)
        running_sum = running_sum + cheb_coef[degree] * current
    return running_sum


def full_matrix(weights_all, offsets_all):
    point_count = weights_all.shape[0]
    positions = jnp.arange(point_count, dtype=jnp.int32)
    target = positions[:, None] + offsets_all
    dense_operator_matrix = jnp.zeros((point_count, point_count), jnp.float32)
    for column in range(weights_all.shape[1]):
        hit = (target[:, column][:, None] == positions[None, :]).astype(jnp.float32)
        dense_operator_matrix = dense_operator_matrix + weights_all[:, column][:, None] * hit
    return dense_operator_matrix


def plain(vectors, kernel_hat, noise_prec, stencil_coefficients_raw, offsets, amplitude, cheb_coef):
    length = vectors.shape[2]
    freq_block = kernel_hat.shape[1]
    padded = freq_block * lax.axis_size("pts")
    forward_operator, inverse = transform_tables(length, padded)
    weights = stencil_coefficients_raw / jnp.sum(stencil_coefficients_raw, axis=1, keepdims=True)
    kernel_real = kernel_hat[0]
    kernel_imag = kernel_hat[1]
    offsets_all = lax.all_gather(offsets, "pts", axis=0, tiled=True)
    weights_all, amplitude_all = (
        lax.all_gather(weights, "pts", axis=0, tiled=True),
        lax.all_gather(amplitude, "pts", axis=0, tiled=True),
    )
    dense_operator_matrix = full_matrix(weights_all, offsets_all)

    def forward_mean(values):
        return jnp.einsum(
            "vcfq,pq->vcfp", values, dense_operator_matrix, precision=exact_evaluation_flag
        )

    def backward_mean(values):
        return jnp.einsum(
            "vcfp,pq->vcfq", values, dense_operator_matrix, precision=exact_evaluation_flag
        )

    source = to_spectrum(vectors, forward_operator)
    spectrum = lax.all_to_all(source, "pts", split_axis=2, concat_axis=3, tiled=True)
    spectrum = amplitude_all[None, None, None, :] * chebyshev(spectrum, forward_mean, cheb_coef)
    real_part = spectrum[:, 0]
    imag_part = spectrum[:, 1]
    data_real = jnp.einsum(
        "fsp,vfp->vfs", kernel_real, real_part, precision=exact_evaluation_flag
    ) - jnp.einsum("fsp,vfp->vfs", kernel_imag, imag_part, precision=exact_evaluation_flag)
    data_imag = jnp.einsum(
        "fsp,vfp->vfs", kernel_real, imag_part, precision=exact_evaluation_flag
    ) + jnp.einsum("fsp,vfp->vfs", kernel_imag, real_part, precision=exact_evaluation_flag)
    data_spec = jnp.stack([data_real, data_imag], axis=1)
    time_series_values = (
        jnp.einsum(
            "rklu,klq->ruq",
            lax.all_to_all(data_spec, "pts", split_axis=3, concat_axis=2, tiled=True),
            inverse,
            precision=exact_evaluation_flag,
        )
        * noise_prec[None, :, None]
    )
    weighted_result = jnp.einsum(
        "lew,jkw->ljke", time_series_values, forward_operator, precision=exact_evaluation_flag
    )
    weighted_result = lax.all_to_all(
        weighted_result, "pts", split_axis=2, concat_axis=3, tiled=True
    )
    back_real = weighted_result[:, 0]
    back_imag = weighted_result[:, 1]
    grad_real = jnp.einsum(
        "fsp,vfs->vfp", kernel_real, back_real, precision=exact_evaluation_flag
    ) + jnp.einsum("fsp,vfs->vfp", kernel_imag, back_imag, precision=exact_evaluation_flag)
    grad_imag = jnp.einsum(
        "fsp,vfs->vfp", kernel_real, back_imag, precision=exact_evaluation_flag
    ) - jnp.einsum("fsp,vfs->vfp", kernel_imag, back_real, precision=exact_evaluation_flag)
    partial_value = chebyshev(
        amplitude_all[None, None, None, :] * jnp.stack([grad_real, grad_imag], axis=1),
        backward_mean,
        cheb_coef,
    )
    summed = lax.psum(partial_value, "sens")
    moved = lax.all_to_all(summed, "pts", split_axis=3, concat_axis=2, tiled=True)
    gradient = to_series(moved, inverse)
    return vectors + gradient


BF = jnp.bfloat16
F32 = jnp.float32
MESH = pl.DeviceIdType.MESH


def up(size, multiple):
    return -(-size // multiple) * multiple


def host_tables(length, block, blocks, padded_block, lanes, padded_time):
    period = 2 * length
    forward = np.zeros((padded_time, blocks, lanes))
    inverse = np.zeros((blocks, lanes, padded_time))
    time = np.arange(length)
    for index in range(blocks):
        frequency = index * block + np.arange(block)
        angle = 2.0 * np.pi / period * (frequency[:, None] * time[None, :] % period)
        active = (frequency <= length)[:, None]
        edge = (frequency == 0) | (frequency == length)
        weight = np.where(edge, 1.0, 2.0)[:, None] / period
        for part, table in enumerate((np.cos(angle) * active, -np.sin(angle) * active)):
            at = slice(part * padded_block, part * padded_block + block)
            forward[:length, index, at] = table.T
            inverse[index, at, :length] = table * weight
    forward = forward.reshape(padded_time, blocks // 2, 2 * lanes).transpose(1, 0, 2)
    inverse = inverse.reshape(blocks // 2, 2 * lanes, padded_time)
    halves = []
    for table in (forward, inverse):
        high = table.astype(ml_dtypes.bfloat16)
        low = (table - high.astype(np.float64)).astype(ml_dtypes.bfloat16)
        halves.append(np.stack([high, low]))
    return halves


def split(values):
    high = values.astype(BF)
    return high, (values - high.astype(F32)).astype(BF)


NN = (((1,), (0,)), ((), ()))
NT = (((1,), (1,)), ((), ()))


def dot3(left, right_high, right_low, dims=NN):
    rows = left.shape[0]
    high, low = split(left)
    both = lax.dot_general(
        jnp.concatenate([high, low], axis=0), right_high, dims, preferred_element_type=F32
    )
    cross = lax.dot_general(high, right_low, dims, preferred_element_type=F32)
    return both[:rows] + both[rows:] + cross


def flip(index, step, size):
    flipped, bit = 0, 1
    while bit < size:
        digit = lax.rem(index // bit, 2)
        flipped = flipped + bit * ((1 - digit) if step & bit else digit)
        bit *= 2
    return flipped


def fused_kernel(
    sizes,
    vec, kern, noise, raw, offs, amp, cheb, fwd_in, inv_in,
    out,
    fwd, inv, k_f32, k_hl, kt_hl, v_own, v_pad, pack, a_send, x_all, spec, y_buf, d_send, d_recv,
    e_send, e_recv, l_buf, g_buf, r_recv, h_send, h_recv, o_buf,
    load_sem, pack_s, pack_r, a_s, a_r, f_s, f_r, d_s, d_r, e_s, e_r, g_s, g_r, h_s, h_r, o_s, o_r,
):
    nv, n_sens, n_pts, fb, fbp, cfp, sl, sq, pt, ple, length, tp = sizes
    me_s = lax.axis_index("sens")
    me_p = lax.axis_index("pts")
    rows = 2 * nv
    pairs = n_pts // 2
    my_pair = me_p // 2
    pts_steps = range(1, n_pts)
    sens_steps = range(1, n_sens)
    pts_peer = [flip(me_p, step, n_pts) for step in range(n_pts)]
    sens_peer = [flip(me_s, step, n_sens) for step in range(n_sens)]
    pair_peer = [flip(my_pair, step, pairs) for step in range(pairs)]

    loads = [
        pltpu.make_async_copy(vec.at[me_s], v_own, load_sem.at[0]),
        pltpu.make_async_copy(fwd_in, fwd, load_sem.at[1]),
        pltpu.make_async_copy(kern.at[0], k_f32.at[0], load_sem.at[2]),
        pltpu.make_async_copy(kern.at[1], k_f32.at[1], load_sem.at[3]),
        pltpu.make_async_copy(inv_in, inv, load_sem.at[4]),
    ]
    loads[0].start()
    loads[1].start()

    barrier = pltpu.get_barrier_semaphore()
    for step in pts_steps:
        pl.semaphore_signal(
            barrier, inc=1, device_id=(me_s, pts_peer[step]), device_id_type=MESH
        )
    for step in sens_steps:
        pl.semaphore_signal(
            barrier, inc=1, device_id=(sens_peer[step], me_p), device_id_type=MESH
        )

    started = []

    def copy_pts(step, src, dst, send_sem, recv_sem):
        return pltpu.make_async_remote_copy(
            src_ref=src, dst_ref=dst, send_sem=send_sem.at[step], recv_sem=recv_sem.at[step],
            device_id=(me_s, pts_peer[step]), device_id_type=MESH,
        )

    def copy_sens(step, slot, src, dst, send_sem, recv_sem):
        at = slot * n_sens + step
        return pltpu.make_async_remote_copy(
            src_ref=src, dst_ref=dst, send_sem=send_sem.at[at], recv_sem=recv_sem.at[at],
            device_id=(sens_peer[step], me_p), device_id_type=MESH,
        )

    def go(copy):
        copy.start()
        started.append(copy)

    nb = raw.shape[0]
    pack[me_p] = jnp.zeros(pack.shape[1:], F32)
    raw_t = raw[...]
    pack[me_p, 0:nb, 0:ple] = raw_t / jnp.sum(raw_t, axis=0, keepdims=True)
    pack[me_p, nb : nb + 1, 0:ple] = amp[...]
    pack[me_p, 0:nb, ple : 2 * ple] = offs[...].astype(F32)

    v_pad[...] = jnp.zeros(v_pad.shape, F32)
    loads[0].wait()
    v_pad[:, 0:length] = v_own[...]
    loads[1].wait()
    for load in loads[2:]:
        load.start()
    pl.semaphore_wait(barrier, n_pts - 1 + n_sens - 1)

    for step in pts_steps:
        go(copy_pts(step, pack.at[me_p], pack.at[me_p], pack_s, pack_r))

    high, low = split(v_pad[...])
    both = jnp.concatenate([high, low], axis=0)
    for turn in list(range(1, pairs)) + [0]:
        pair = pair_peer[turn]
        part = jnp.dot(both, fwd[0, pair], preferred_element_type=F32)
        source = part[:ple] + part[ple:] + jnp.dot(high, fwd[1, pair], preferred_element_type=F32)
        for side in range(2):
            a_send[2 * pair + side] = source[:, side * cfp : (side + 1) * cfp]
        for step in (2 * turn, 2 * turn + 1):
            if step:
                go(copy_pts(step, a_send.at[pts_peer[step]], x_all.at[me_s, me_p], a_s, a_r))
    x_all[me_s, me_p] = a_send[me_p]

    def hand_on(step):
        for other in sens_steps:
            block = x_all.at[me_s, pts_peer[step]]
            go(copy_sens(other, step, block, block, f_s, f_r))

    hand_on(0)

    loads[2].wait()
    loads[3].wait()

    def halve(index, carry):
        high, low = split(jnp.concatenate([k_f32[0, index], k_f32[1, index]], axis=0))
        k_hl[index, 0 : 2 * sl] = high
        k_hl[index, 2 * sl : 4 * sl] = low
        return carry

    def halve_turned(index, carry):
        both = jnp.concatenate([k_f32[0, index], k_f32[1, index]], axis=0)
        high, low = split(jnp.transpose(both))
        kt_hl[index, :, 0 : 2 * sl] = high
        kt_hl[index, :, 2 * sl : 4 * sl] = low
        return carry

    share = -(-fb // (n_pts - 1))
    for step in pts_steps:
        lax.fori_loop(min((step - 1) * share, fb), min(step * share, fb), halve, 0, unroll=2)
        block = x_all.at[me_s, pts_peer[step]]
        copy_pts(step, block, block, a_s, a_r).wait_recv()
        hand_on(step)
    for index in range(fb, fbp):
        k_hl[index] = jnp.zeros(k_hl.shape[1:], BF)
        kt_hl[index] = jnp.zeros(kt_hl.shape[1:], BF)

    for step in pts_steps:
        block = pack.at[pts_peer[step]]
        copy_pts(step, block, block, pack_s, pack_r).wait_recv()
    gathered = [pack[index] for index in range(n_pts)]
    weights_row = jnp.concatenate([block[:, 0:ple] for block in gathered], axis=1)
    offsets_row = jnp.concatenate([block[:, ple : 2 * ple] for block in gathered], axis=1)
    down = lax.broadcasted_iota(jnp.int32, (pt, pt), 0)
    across = lax.broadcasted_iota(jnp.int32, (pt, pt), 1)
    shift = (down - across).astype(F32)
    mean_t = jnp.zeros((pt, pt), F32)
    for k in range(nb):
        mean_t = mean_t + jnp.where(
            shift == offsets_row[k : k + 1], weights_row[k : k + 1], 0.0
        )
    identity = jnp.where(down == across, 1.0, 0.0).astype(F32)
    before, now = identity, mean_t
    total = cheb[0] * before + cheb[1] * now
    mean_h, mean_l = split(mean_t)
    for degree in range(2, cheb.shape[0]):
        before, now = now, 2.0 * dot3(now, mean_h, mean_l) - before
        total = total + cheb[degree] * now
    prior_t = total * weights_row[nb : nb + 1]
    prior_h, prior_l = split(prior_t)

    for other in range(n_sens):
        v = sens_peer[other]
        if other:
            for step in range(n_pts):
                block = x_all.at[v, pts_peer[step]]
                copy_sens(other, step, block, block, f_s, f_r).wait_recv()
        own = dot3(jnp.transpose(x_all[v].reshape(pt, cfp)), prior_h, prior_l)
        for part in range(2):
            spec[part, v] = own[part * fbp : (part + 1) * fbp]

    lane = lax.broadcasted_iota(jnp.int32, (1, 16 * rows), 1)
    lane_of = lax.rem(lane, 8)
    sign = jnp.where(lax.rem(lane // (8 * nv), 2) == 0, -1.0, 1.0).astype(F32)

    def columns(values):
        high = values.astype(BF).astype(F32)
        return jnp.transpose(jnp.concatenate([high, values - high], axis=0)).astype(BF)

    def keep_own(products):
        kept = products[0]
        for index in range(1, 8):
            kept = jnp.where(lane_of == index, products[index], kept)
        return kept + pltpu.roll(kept, 8 * rows, 1)

    for group in range(fbp // 8):
        at = 8 * group
        weight = columns(
            jnp.concatenate(
                [spec[part, v, at : at + 8] for part in range(2) for v in range(nv)], axis=0
            )
        )
        product = jnp.dot(
            k_hl[at : at + 8].reshape(32 * sl, pt), weight, preferred_element_type=F32
        ).reshape(8, 2, 2 * sl, 16 * rows)
        kept = keep_own([product[index, 0] + product[index, 1] for index in range(8)])
        data = kept[:sl] + sign * pltpu.roll(kept[sl:], 8 * nv, 1)
        y_buf[group] = jnp.transpose(data)[: 8 * rows].reshape(rows, 8, sl)

    blank = jnp.zeros((cfp - 2 * fbp, sl), F32)
    for v in range(nv):
        data = jnp.transpose(
            jnp.concatenate(
                [y_buf[group, part * nv + v] for part in range(2) for group in range(fbp // 8)]
                + [blank],
                axis=0,
            )
        )
        for index in range(n_pts):
            d_send[index, v] = data[index * sq : (index + 1) * sq]
    for step in reversed(pts_steps):
        go(copy_pts(step, d_send.at[pts_peer[step]], d_recv.at[me_p], d_s, d_r))
    d_recv[me_p] = d_send[me_p]
    lax.fori_loop(0, fb // 2, halve_turned, 0, unroll=2)
    loads[4].wait()
    which = lax.rem(lax.broadcasted_iota(jnp.int32, (nv * sq, 1), 0), sq)
    precision = jnp.zeros((nv * sq, 1), F32)
    for index in range(sq):
        precision = jnp.where(which == index, noise[index], precision)

    def series(received, lines, send_sem, recv_sem):
        result = jnp.zeros((lines, tp), F32)
        for turn in range(pairs):
            for step in (2 * turn, 2 * turn + 1):
                if step:
                    block = received.at[pts_peer[step]]
                    copy_pts(step, block, block, send_sem, recv_sem).wait_recv()
            pair = pair_peer[turn]
            both = jnp.concatenate(
                [received[2 * pair + side].reshape(lines, cfp) for side in range(2)], axis=1
            )
            result = result + dot3(both, inv[0, pair], inv[1, pair])
        return result

    data = series(d_recv, nv * sq, d_s, d_r) * precision
    high, low = split(data)
    both = jnp.concatenate([high, low], axis=0)
    lines = nv * sq
    for turn in list(range(1, pairs)) + [0]:
        pair = pair_peer[turn]
        part = jnp.dot(both, fwd[0, pair], preferred_element_type=F32)
        back = part[:lines] + part[lines:] + jnp.dot(high, fwd[1, pair], preferred_element_type=F32)
        for side in range(2):
            e_send[2 * pair + side] = back[:, side * cfp : (side + 1) * cfp].reshape(nv, sq, cfp)
        for step in (2 * turn, 2 * turn + 1):
            if step:
                go(copy_pts(step, e_send.at[pts_peer[step]], e_recv.at[me_p], e_s, e_r))
    e_recv[me_p] = e_send[me_p]
    lax.fori_loop(fb // 2, fb, halve_turned, 0, unroll=2)
    for step in pts_steps:
        block = e_recv.at[pts_peer[step]]
        copy_pts(step, block, block, e_s, e_r).wait_recv()
    for v in range(nv):
        turned = jnp.transpose(
            jnp.concatenate([e_recv[index, v] for index in range(n_pts)], axis=0)
        )
        real, imag = turned[:fbp], turned[fbp : 2 * fbp]
        l_buf[0, v] = jnp.concatenate([real, imag], axis=1)
        l_buf[1, v] = jnp.concatenate([imag, -real], axis=1)

    groups = [(at, min(16, fbp - at)) for at in range(0, fbp, 16)]
    for slot, (at, count) in enumerate(groups):
        for first in range(at, at + count, 8):
            weight = columns(l_buf[:, :, first : first + 8].reshape(8 * rows, 2 * sl))
            product = jnp.dot(
                kt_hl[first : first + 8].reshape(8 * pt, 4 * sl),
                jnp.concatenate([weight, weight], axis=0),
                preferred_element_type=F32,
            ).reshape(8, pt, 16 * rows)
            kept = jnp.transpose(keep_own([product[index] for index in range(8)]))
            for part in range(2):
                for v in range(nv):
                    row = 8 * (part * nv + v)
                    g_buf[part, v, first : first + 8] = kept[row : row + 8]
        for step in reversed(sens_steps):
            go(
                copy_sens(
                    step, slot,
                    g_buf.at[:, sens_peer[step], pl.ds(at, count), :],
                    r_recv.at[me_s, :, pl.ds(at, count), :],
                    g_s, g_r,
                )
            )
    gradient = g_buf[:, me_s]
    for slot, (at, count) in enumerate(groups):
        for step in sens_steps:
            block = r_recv.at[sens_peer[step], :, pl.ds(at, count), :]
            copy_sens(step, slot, block, block, g_s, g_r).wait_recv()
    for step in sens_steps:
        gradient = gradient + r_recv[sens_peer[step]]
    gradient = jnp.concatenate(
        [gradient.reshape(2 * fbp, pt), jnp.zeros((cfp - 2 * fbp, pt), F32)], axis=0
    )
    grad_h, grad_l = split(gradient)
    h_send[...] = dot3(prior_t, grad_h, grad_l, NT).reshape(h_send.shape)
    for step in reversed(pts_steps):
        go(copy_pts(step, h_send.at[pts_peer[step]], h_recv.at[me_p], h_s, h_r))
    h_recv[me_p] = h_send[me_p]
    o_buf[me_s] = series(h_recv, ple, h_s, h_r)
    for step in reversed(sens_steps):
        go(copy_sens(step, 0, o_buf.at[me_s], o_buf.at[me_s], o_s, o_r))
    out[me_s] = o_buf[me_s, :, 0:length]
    for step in sens_steps:
        block = o_buf.at[sens_peer[step]]
        copy_sens(step, 0, block, block, o_s, o_r).wait_recv()
        out[sens_peer[step]] = o_buf[sens_peer[step], :, 0:length]
    for copy in started:
        copy.wait_send()


def local(vectors, kernel_hat, noise_prec, stencil_coefficients_raw, offsets, amplitude, cheb_coef):
    n_sens, n_pts = lax.axis_size("sens"), lax.axis_size("pts")
    nv, ple, length = vectors.shape
    fb, sl, pt = kernel_hat.shape[1:]
    nb = offsets.shape[1]
    fbp = up(fb, 8)
    cfp = up(2 * fbp, 128)
    tp = up(length, 128)
    sq = sl // n_pts
    fits = (
        nv == n_sens
        and 2 * nv == 8
        and n_pts & (n_pts - 1) == 0
        and n_pts > 1
        and nb < 8
        and ple % 8 == 0
        and 2 * ple <= 128
        and sl == sq * n_pts
        and sq % 8 == 0
        and 2 * sl == 128
        and pt % 128 == 0
        and kernel_hat.size < 2**21
    )
    if not fits:
        return plain(
            vectors, kernel_hat, noise_prec, stencil_coefficients_raw, offsets, amplitude, cheb_coef
        )
    forward, inverse = host_tables(length, fb, n_pts, fbp, cfp, tp)
    sizes = (nv, n_sens, n_pts, fb, fbp, cfp, sl, sq, pt, ple, length, tp)
    vmem = pl.BlockSpec(memory_space=pltpu.VMEM)
    smem = pl.BlockSpec(memory_space=pltpu.SMEM)
    anywhere = pl.BlockSpec(memory_space=pl.ANY)

    def f32(*shape):
        return pltpu.VMEM(shape, F32)

    def sems(count):
        return pltpu.SemaphoreType.DMA((count,))

    gradient = pl.pallas_call(
        functools.partial(fused_kernel, sizes),
        out_shape=jax.ShapeDtypeStruct(vectors.shape, F32),
        in_specs=[anywhere, anywhere, smem, vmem, vmem, vmem, smem, anywhere, anywhere],
        out_specs=vmem,
        scratch_shapes=[
            pltpu.VMEM(forward.shape, BF),
            pltpu.VMEM(inverse.shape, BF),
            f32(2, fb, sl, pt),
            pltpu.VMEM((fbp, 4 * sl, pt), BF),
            pltpu.VMEM((fbp, pt, 4 * sl), BF),
            f32(ple, length),
            f32(ple, tp),
            f32(n_pts, 8, 128),
            f32(n_pts, ple, cfp),
            f32(nv, n_pts, ple, cfp),
            f32(2, nv, fbp, pt),
            f32(fbp // 8, 2 * nv, 8, sl),
            f32(n_pts, nv, sq, cfp),
            f32(n_pts, nv, sq, cfp),
            f32(n_pts, nv, sq, cfp),
            f32(n_pts, nv, sq, cfp),
            f32(2, nv, fbp, 2 * sl),
            f32(2, nv, fbp, pt),
            f32(n_sens, 2, fbp, pt),
            f32(n_pts, ple, cfp),
            f32(n_pts, ple, cfp),
            f32(nv, ple, tp),
            sems(5),
            *[sems(n_pts)] * 4,
            *[sems(n_pts * n_sens)] * 2,
            *[sems(n_pts)] * 4,
            *[sems(up(fbp, 16) // 16 * n_sens)] * 2,
            *[sems(n_pts)] * 2,
            *[sems(n_sens)] * 2,
        ],
        compiler_params=pltpu.CompilerParams(
            collective_id=0, has_side_effects=True, vmem_limit_bytes=56 * 2**20
        ),
    )(
        vectors, kernel_hat, noise_prec, stencil_coefficients_raw.T, offsets.T,
        amplitude.reshape(1, ple), cheb_coef, forward, inverse,
    )
    return vectors + gradient


def solution(mesh):
    placed = (
        P(None, "pts", None),
        P(None, "pts", "sens", None),
        P(("sens", "pts")),
        P("pts", None),
        P("pts", None),
        P("pts"),
        P(),
    )
    return jax.shard_map(
        local, mesh=mesh, in_specs=placed, out_specs=P(None, "pts", None), check_vma=False
    )
```

```python
import functools

import jax
import jax.numpy as jnp
import ml_dtypes
import numpy as np
from jax import lax
from jax.experimental import pallas as pl
from jax.experimental.pallas import tpu as pltpu
from jax.sharding import PartitionSpec as P

exact_evaluation_flag = lax.Precision.HIGHEST


def transform_tables(length, padded):
    time_index = jnp.arange(length, dtype=jnp.int32)
    frequency = jnp.arange(padded, dtype=jnp.int32)
    period = 2 * length
    phase_index = frequency[:, None] * time_index[None, :] % period
    angles = 2.0 * jnp.pi / period * phase_index.astype(jnp.float32)
    active = (frequency <= length).astype(jnp.float32)[:, None]
    cosine = jnp.cos(angles)
    sine_part = jnp.sin(angles)
    forward_operator = jnp.stack([cosine * active, -sine_part * active])
    edge_rows = (frequency == 0) | (frequency == length)
    weight = jnp.where(edge_rows, 1.0, 2.0).astype(jnp.float32)[:, None] * active / period
    inverse = jnp.stack([cosine * weight, -sine_part * weight])
    return (forward_operator, inverse)


def to_spectrum(time_series_values, forward_operator):
    return jnp.einsum(
        "vpt,cft->vcfp", time_series_values, forward_operator, precision=exact_evaluation_flag
    )


def to_series(spectrum, inverse):
    return jnp.einsum("vcfp,cft->vpt", spectrum, inverse, precision=exact_evaluation_flag)


def chebyshev(values_in, operator, cheb_coef):
    previous = values_in
    current = operator(values_in)
    running_sum = cheb_coef[0] * previous + cheb_coef[1] * current
    for degree in range(2, cheb_coef.shape[0]):
        following = 2.0 * operator(current) - previous
        previous, current = (current, following)
        running_sum = running_sum + cheb_coef[degree] * current
    return running_sum


def full_matrix(weights_all, offsets_all):
    point_count = weights_all.shape[0]
    positions = jnp.arange(point_count, dtype=jnp.int32)
    target = positions[:, None] + offsets_all
    dense_operator_matrix = jnp.zeros((point_count, point_count), jnp.float32)
    for column in range(weights_all.shape[1]):
        hit = (target[:, column][:, None] == positions[None, :]).astype(jnp.float32)
        dense_operator_matrix = dense_operator_matrix + weights_all[:, column][:, None] * hit
    return dense_operator_matrix


def plain(vectors, kernel_hat, noise_prec, stencil_coefficients_raw, offsets, amplitude, cheb_coef):
    length = vectors.shape[2]
    freq_block = kernel_hat.shape[1]
    padded = freq_block * lax.axis_size("pts")
    forward_operator, inverse = transform_tables(length, padded)
    weights = stencil_coefficients_raw / jnp.sum(stencil_coefficients_raw, axis=1, keepdims=True)
    kernel_real = kernel_hat[0]
    kernel_imag = kernel_hat[1]
    offsets_all = lax.all_gather(offsets, "pts", axis=0, tiled=True)
    weights_all, amplitude_all = (
        lax.all_gather(weights, "pts", axis=0, tiled=True),
        lax.all_gather(amplitude, "pts", axis=0, tiled=True),
    )
    dense_operator_matrix = full_matrix(weights_all, offsets_all)

    def forward_mean(values):
        return jnp.einsum(
            "vcfq,pq->vcfp", values, dense_operator_matrix, precision=exact_evaluation_flag
        )

    def backward_mean(values):
        return jnp.einsum(
            "vcfp,pq->vcfq", values, dense_operator_matrix, precision=exact_evaluation_flag
        )

    source = to_spectrum(vectors, forward_operator)
    spectrum = lax.all_to_all(source, "pts", split_axis=2, concat_axis=3, tiled=True)
    spectrum = amplitude_all[None, None, None, :] * chebyshev(spectrum, forward_mean, cheb_coef)
    real_part = spectrum[:, 0]
    imag_part = spectrum[:, 1]
    data_real = jnp.einsum(
        "fsp,vfp->vfs", kernel_real, real_part, precision=exact_evaluation_flag
    ) - jnp.einsum("fsp,vfp->vfs", kernel_imag, imag_part, precision=exact_evaluation_flag)
    data_imag = jnp.einsum(
        "fsp,vfp->vfs", kernel_real, imag_part, precision=exact_evaluation_flag
    ) + jnp.einsum("fsp,vfp->vfs", kernel_imag, real_part, precision=exact_evaluation_flag)
    data_spec = jnp.stack([data_real, data_imag], axis=1)
    time_series_values = (
        jnp.einsum(
            "rklu,klq->ruq",
            lax.all_to_all(data_spec, "pts", split_axis=3, concat_axis=2, tiled=True),
            inverse,
            precision=exact_evaluation_flag,
        )
        * noise_prec[None, :, None]
    )
    weighted_result = jnp.einsum(
        "lew,jkw->ljke", time_series_values, forward_operator, precision=exact_evaluation_flag
    )
    weighted_result = lax.all_to_all(
        weighted_result, "pts", split_axis=2, concat_axis=3, tiled=True
    )
    back_real = weighted_result[:, 0]
    back_imag = weighted_result[:, 1]
    grad_real = jnp.einsum(
        "fsp,vfs->vfp", kernel_real, back_real, precision=exact_evaluation_flag
    ) + jnp.einsum("fsp,vfs->vfp", kernel_imag, back_imag, precision=exact_evaluation_flag)
    grad_imag = jnp.einsum(
        "fsp,vfs->vfp", kernel_real, back_imag, precision=exact_evaluation_flag
    ) - jnp.einsum("fsp,vfs->vfp", kernel_imag, back_real, precision=exact_evaluation_flag)
    partial_value = chebyshev(
        amplitude_all[None, None, None, :] * jnp.stack([grad_real, grad_imag], axis=1),
        backward_mean,
        cheb_coef,
    )
    summed = lax.psum(partial_value, "sens")
    moved = lax.all_to_all(summed, "pts", split_axis=3, concat_axis=2, tiled=True)
    gradient = to_series(moved, inverse)
    return vectors + gradient


BF = jnp.bfloat16
F32 = jnp.float32
MESH = pl.DeviceIdType.MESH


def up(size, multiple):
    return -(-size // multiple) * multiple


def host_tables(length, block, blocks, padded_block, lanes, padded_time):
    period = 2 * length
    forward = np.zeros((padded_time, blocks, lanes))
    inverse = np.zeros((blocks, lanes, padded_time))
    time = np.arange(length)
    for index in range(blocks):
        frequency = index * block + np.arange(block)
        angle = 2.0 * np.pi / period * (frequency[:, None] * time[None, :] % period)
        active = (frequency <= length)[:, None]
        edge = (frequency == 0) | (frequency == length)
        weight = np.where(edge, 1.0, 2.0)[:, None] / period
        for part, table in enumerate((np.cos(angle) * active, -np.sin(angle) * active)):
            at = slice(part * padded_block, part * padded_block + block)
            forward[:length, index, at] = table.T
            inverse[index, at, :length] = table * weight
    forward = forward.reshape(padded_time, blocks // 2, 2 * lanes).transpose(1, 0, 2)
    inverse = inverse.reshape(blocks // 2, 2 * lanes, padded_time)
    halves = []
    for table in (forward, inverse):
        high = table.astype(ml_dtypes.bfloat16)
        low = (table - high.astype(np.float64)).astype(ml_dtypes.bfloat16)
        halves.append(np.stack([high, low], axis=1))
    return halves


def split(values):
    high = values.astype(BF)
    return high, (values - high.astype(F32)).astype(BF)


NN = (((1,), (0,)), ((), ()))
NT = (((1,), (1,)), ((), ()))


def dot3(left, right_high, right_low, dims=NN):
    rows = left.shape[0]
    high, low = split(left)
    both = lax.dot_general(
        jnp.concatenate([high, low], axis=0), right_high, dims, preferred_element_type=F32
    )
    cross = lax.dot_general(high, right_low, dims, preferred_element_type=F32)
    return both[:rows] + both[rows:] + cross


def flip(index, step, size):
    flipped, bit = 0, 1
    while bit < size:
        digit = lax.rem(index // bit, 2)
        flipped = flipped + bit * ((1 - digit) if step & bit else digit)
        bit *= 2
    return flipped


def fused_kernel(
    sizes,
    vec, kern, noise, raw, offs, amp, cheb, fwd_in, inv_in,
    out,
    fwd, inv, k_f32, k_hl, kt_hl, v_in, v_pad, a_send, a_recv, b_send, x_all, spec, y_buf,
    d_send, d_recv, e_send, e_recv, l_buf, g_buf, r_recv, h_send, h_recv, o_buf,
    load_sem, fwd_sem, a_s, a_r, b_s, b_r, f_s, f_r, d_s, d_r, e_s, e_r, g_s, g_r, h_s, h_r, o_s, o_r,
):
    nv, n_sens, n_pts, fb, fbp, cfp, sl, sq, pt, ple, length, tp = sizes
    me_s = lax.axis_index("sens")
    me_p = lax.axis_index("pts")
    rows = 2 * nv
    pairs = n_pts // 2
    pts_steps = range(1, n_pts)
    sens_steps = range(1, n_sens)
    far_first = list(range(pairs - 1, -1, -1))
    pts_peer = [flip(me_p, step, n_pts) for step in range(n_pts)]
    sens_peer = [flip(me_s, step, n_sens) for step in range(n_sens)]
    pair_peer = [flip(me_p // 2, step, pairs) for step in range(pairs)]

    vec_load = pltpu.make_async_copy(vec, v_in, load_sem.at[0])
    k_loads = [
        pltpu.make_async_copy(kern.at[part], k_f32.at[part], load_sem.at[1 + part])
        for part in range(2)
    ]
    inv_load = pltpu.make_async_copy(inv_in, inv, load_sem.at[3])
    fwd_loads = [
        pltpu.make_async_copy(fwd_in.at[pair], fwd.at[pair], fwd_sem.at[turn])
        for turn, pair in enumerate(pair_peer)
    ]
    vec_load.start()
    for turn in far_first:
        fwd_loads[turn].start()

    barrier = pltpu.get_barrier_semaphore()
    for step in pts_steps:
        pl.semaphore_signal(
            barrier, inc=1, device_id=(me_s, pts_peer[step]), device_id_type=MESH
        )
    for step in sens_steps:
        pl.semaphore_signal(
            barrier, inc=1, device_id=(sens_peer[step], me_p), device_id_type=MESH
        )

    def to_pts(step, src, dst, send_sem, recv_sem):
        pltpu.make_async_remote_copy(
            src_ref=src, dst_ref=dst, send_sem=send_sem, recv_sem=recv_sem.at[step // 2],
            device_id=(me_s, pts_peer[step]), device_id_type=MESH,
        ).start()

    def to_sens(step, src, dst, send_sem, recv_sem):
        pltpu.make_async_remote_copy(
            src_ref=src, dst_ref=dst, send_sem=send_sem, recv_sem=recv_sem.at[step],
            device_id=(sens_peer[step], me_p), device_id_type=MESH,
        ).start()

    def wait(block, semaphore):
        pltpu.make_async_copy(block, block, semaphore).wait()

    def wait_pair(turn, received, semaphore):
        if turn:
            wait(received.at[pl.ds(2 * pair_peer[turn], 2)], semaphore.at[turn])
        else:
            wait(received.at[pts_peer[1]], semaphore.at[0])

    nb = raw.shape[0]
    raw_t = raw[...]
    pack = jnp.concatenate(
        [
            jnp.concatenate(
                [raw_t / jnp.sum(raw_t, axis=0, keepdims=True), offs[...].astype(F32)], axis=1
            ),
            jnp.concatenate([amp[...], amp[...]], axis=1),
            jnp.zeros((7 - nb, 2 * ple), F32),
        ],
        axis=0,
    )
    for index in range(n_pts):
        a_send[index, ple:] = jnp.zeros((8, cfp), F32)
        a_send[index, ple:, 0 : 2 * ple] = pack

    v_pad[...] = jnp.zeros(v_pad.shape, F32)
    vec_load.wait()
    v_pad[:, :, 0:length] = v_in[...]

    def transformed(values, pair, lines):
        high, low = split(values)
        both = jnp.concatenate([high, low], axis=0)
        part = jnp.dot(both, fwd[pair, 0], preferred_element_type=F32)
        return (
            part[:lines] + part[lines:]
            + jnp.dot(high, fwd[pair, 1], preferred_element_type=F32)
        )

    mine = v_pad[me_s]
    for turn in far_first:
        pair = pair_peer[turn]
        fwd_loads[turn].wait()
        if turn == pairs - 1:
            pl.semaphore_wait(barrier, n_pts - 1 + n_sens - 1)
        if turn:
            source = transformed(mine, pair, ple)
            for side in range(2):
                a_send[2 * pair + side, 0:ple] = source[:, side * cfp : (side + 1) * cfp]
            for step in (2 * turn, 2 * turn + 1):
                to_pts(step, a_send.at[pts_peer[step]], a_recv.at[me_p], a_s, a_r)
    for load in k_loads:
        load.start()
    inv_load.start()
    source = transformed(v_pad[...].reshape(nv * ple, tp), pair_peer[0], nv * ple)
    for side in range(2):
        b_send[side] = source[:, side * cfp : (side + 1) * cfp].reshape(nv, ple, cfp)
    other_side = lax.rem(pts_peer[1], 2)
    to_pts(1, b_send.at[other_side], x_all.at[:, me_p], b_s.at[0], b_r)
    to_pts(1, a_send.at[pts_peer[1], ple:], a_recv.at[me_p, ple:], b_s.at[1], a_r)
    own_side = lax.rem(me_p, 2)
    for v in range(nv):
        x_all[v, me_p] = b_send[own_side, v]
    a_recv[me_p, ple:] = a_send[me_p, ple:]

    for load in k_loads:
        load.wait()

    def halve(index, carry):
        high, low = split(jnp.concatenate([k_f32[0, index], k_f32[1, index]], axis=0))
        k_hl[index, 0 : 2 * sl] = high
        k_hl[index, 2 * sl : 4 * sl] = low
        return carry

    def halve_turned(index, carry):
        both = jnp.concatenate([k_f32[0, index], k_f32[1, index]], axis=0)
        high, low = split(jnp.transpose(both))
        kt_hl[index, :, 0 : 2 * sl] = high
        kt_hl[index, :, 2 * sl : 4 * sl] = low
        return carry

    share = -(-fb // pairs)
    for turn in list(range(1, pairs)) + [0]:
        first = (turn - 1 if turn else pairs - 1) * share
        lax.fori_loop(min(first, fb), min(first + share, fb), halve, 0, unroll=2)
        if turn:
            wait_pair(turn, a_recv, a_r)
            span = pl.ds(2 * pair_peer[turn], 2)
            for step in sens_steps:
                to_sens(
                    step, a_recv.at[span, 0:ple], x_all.at[me_s, span], f_s, f_r
                )
            for side in range(2):
                at = 2 * pair_peer[turn] + side
                x_all[me_s, at] = a_recv[at, 0:ple]
        else:
            wait(a_recv.at[pts_peer[1], ple:], a_r.at[0])
    for index in range(fb, fbp):
        k_hl[index] = jnp.zeros(k_hl.shape[1:], BF)
        kt_hl[index] = jnp.zeros(kt_hl.shape[1:], BF)

    gathered = [a_recv[index, ple:] for index in range(n_pts)]
    weights_row = jnp.concatenate([block[:, 0:ple] for block in gathered], axis=1)
    offsets_row = jnp.concatenate([block[:, ple : 2 * ple] for block in gathered], axis=1)
    down = lax.broadcasted_iota(jnp.int32, (pt, pt), 0)
    across = lax.broadcasted_iota(jnp.int32, (pt, pt), 1)
    shift = (down - across).astype(F32)
    mean_t = jnp.zeros((pt, pt), F32)
    for k in range(nb):
        mean_t = mean_t + jnp.where(
            shift == offsets_row[k : k + 1], weights_row[k : k + 1], 0.0
        )
    identity = jnp.where(down == across, 1.0, 0.0).astype(F32)
    before, now = identity, mean_t
    total = cheb[0] * before + cheb[1] * now
    mean_h, mean_l = split(mean_t)
    for degree in range(2, cheb.shape[0]):
        before, now = now, 2.0 * dot3(now, mean_h, mean_l) - before
        total = total + cheb[degree] * now
    prior_t = total * weights_row[nb : nb + 1]
    prior_h, prior_l = split(prior_t)

    wait(x_all.at[:, pts_peer[1]], b_r.at[0])
    for other in range(n_sens):
        v = sens_peer[other]
        if other:
            wait(x_all.at[v, pl.ds(0, n_pts - 2)], f_r.at[other])
        own = dot3(jnp.transpose(x_all[v].reshape(pt, cfp)), prior_h, prior_l)
        for part in range(2):
            spec[part, v] = own[part * fbp : (part + 1) * fbp]

    lane = lax.broadcasted_iota(jnp.int32, (1, 16 * rows), 1)
    lane_of = lax.rem(lane, 8)
    sign = jnp.where(lax.rem(lane // (8 * nv), 2) == 0, -1.0, 1.0).astype(F32)

    def columns(values):
        high = values.astype(BF).astype(F32)
        return jnp.transpose(jnp.concatenate([high, values - high], axis=0)).astype(BF)

    def keep_own(products):
        kept = products[0]
        for index in range(1, 8):
            kept = jnp.where(lane_of == index, products[index], kept)
        return kept + pltpu.roll(kept, 8 * rows, 1)

    for group in range(fbp // 8):
        at = 8 * group
        weight = columns(
            jnp.concatenate(
                [spec[part, v, at : at + 8] for part in range(2) for v in range(nv)], axis=0
            )
        )
        product = jnp.dot(
            k_hl[at : at + 8].reshape(32 * sl, pt), weight, preferred_element_type=F32
        ).reshape(8, 2, 2 * sl, 16 * rows)
        kept = keep_own([product[index, 0] + product[index, 1] for index in range(8)])
        data = kept[:sl] + sign * pltpu.roll(kept[sl:], 8 * nv, 1)
        y_buf[group] = jnp.transpose(data)[: 8 * rows].reshape(rows, 8, sl)

    blank = jnp.zeros((cfp - 2 * fbp, sl), F32)
    for v in range(nv):
        data = jnp.transpose(
            jnp.concatenate(
                [y_buf[group, part * nv + v] for part in range(2) for group in range(fbp // 8)]
                + [blank],
                axis=0,
            )
        )
        for index in range(n_pts):
            d_send[index, v] = data[index * sq : (index + 1) * sq]
    for step in reversed(pts_steps):
        to_pts(step, d_send.at[pts_peer[step]], d_recv.at[me_p], d_s, d_r)
    d_recv[me_p] = d_send[me_p]
    lax.fori_loop(0, fb // 2, halve_turned, 0, unroll=2)
    inv_load.wait()
    which = lax.rem(lax.broadcasted_iota(jnp.int32, (nv * sq, 1), 0), sq)
    precision = jnp.zeros((nv * sq, 1), F32)
    for index in range(sq):
        precision = jnp.where(which == index, noise[index], precision)

    def series(received, lines, recv_sem):
        result = jnp.zeros((lines, tp), F32)
        for turn in range(pairs):
            wait_pair(turn, received, recv_sem)
            pair = pair_peer[turn]
            both = jnp.concatenate(
                [received[2 * pair + side].reshape(lines, cfp) for side in range(2)], axis=1
            )
            result = result + dot3(both, inv[pair, 0], inv[pair, 1])
        return result

    data = series(d_recv, nv * sq, d_r) * precision
    for turn in far_first:
        pair = pair_peer[turn]
        back = transformed(data, pair, nv * sq)
        for side in range(2):
            e_send[2 * pair + side] = back[:, side * cfp : (side + 1) * cfp].reshape(nv, sq, cfp)
        for step in (2 * turn + 1, 2 * turn):
            if step:
                to_pts(step, e_send.at[pts_peer[step]], e_recv.at[me_p], e_s, e_r)
    e_recv[me_p] = e_send[me_p]
    lax.fori_loop(fb // 2, fb, halve_turned, 0, unroll=2)
    for turn in range(pairs):
        wait_pair(turn, e_recv, e_r)
    for v in range(nv):
        turned = jnp.transpose(
            jnp.concatenate([e_recv[index, v] for index in range(n_pts)], axis=0)
        )
        real, imag = turned[:fbp], turned[fbp : 2 * fbp]
        l_buf[0, v] = jnp.concatenate([real, imag], axis=1)
        l_buf[1, v] = jnp.concatenate([imag, -real], axis=1)

    groups = [(at, min(24, fbp - at)) for at in range(0, fbp, 24)]
    for at, count in groups:
        for first in range(at, at + count, 8):
            weight = columns(l_buf[:, :, first : first + 8].reshape(8 * rows, 2 * sl))
            product = jnp.dot(
                kt_hl[first : first + 8].reshape(8 * pt, 4 * sl),
                jnp.concatenate([weight, weight], axis=0),
                preferred_element_type=F32,
            ).reshape(8, pt, 16 * rows)
            kept = jnp.transpose(keep_own([product[index] for index in range(8)]))
            for part in range(2):
                for v in range(nv):
                    row = 8 * (part * nv + v)
                    g_buf[part, v, first : first + 8] = kept[row : row + 8]
        for step in reversed(sens_steps):
            to_sens(
                step,
                g_buf.at[:, sens_peer[step], pl.ds(at, count), :],
                r_recv.at[me_s, :, pl.ds(at, count), :],
                g_s, g_r,
            )
    gradient = g_buf[:, me_s]
    for step in sens_steps:
        wait(r_recv.at[sens_peer[step]], g_r.at[step])
        gradient = gradient + r_recv[sens_peer[step]]
    gradient = jnp.concatenate(
        [gradient.reshape(2 * fbp, pt), jnp.zeros((cfp - 2 * fbp, pt), F32)], axis=0
    )
    grad_h, grad_l = split(gradient)
    h_send[...] = dot3(prior_t, grad_h, grad_l, NT).reshape(h_send.shape)
    for step in reversed(pts_steps):
        to_pts(step, h_send.at[pts_peer[step]], h_recv.at[me_p], h_s, h_r)
    h_recv[me_p] = h_send[me_p]
    o_buf[me_s] = series(h_recv, ple, h_r)
    for step in reversed(sens_steps):
        to_sens(step, o_buf.at[me_s], o_buf.at[me_s], o_s, o_r)
    out[me_s] = o_buf[me_s, :, 0:length]
    for step in sens_steps:
        wait(o_buf.at[sens_peer[step]], o_r.at[step])
        out[sens_peer[step]] = o_buf[sens_peer[step], :, 0:length]

    wait(a_send.at[pl.ds(0, n_pts - 2)], a_s)
    wait(b_send.at[0], b_s.at[0])
    wait(a_send.at[0, ple:], b_s.at[1])
    wait(x_all.at[pl.ds(0, n_sens - 1), pl.ds(0, n_pts - 2)], f_s)
    for sent, semaphore in ((d_send, d_s), (e_send, e_s), (h_send, h_s)):
        wait(sent.at[pl.ds(0, n_pts - 1)], semaphore)
    wait(r_recv.at[pl.ds(0, n_sens - 1)], g_s)
    wait(o_buf.at[pl.ds(0, n_sens - 1)], o_s)


def local(vectors, kernel_hat, noise_prec, stencil_coefficients_raw, offsets, amplitude, cheb_coef):
    n_sens, n_pts = lax.axis_size("sens"), lax.axis_size("pts")
    nv, ple, length = vectors.shape
    fb, sl, pt = kernel_hat.shape[1:]
    nb = offsets.shape[1]
    fbp = up(fb, 8)
    cfp = up(2 * fbp, 128)
    tp = up(length, 128)
    sq = sl // n_pts
    fits = (
        nv == n_sens
        and 2 * nv == 8
        and n_pts & (n_pts - 1) == 0
        and nb < 8
        and n_pts > 2
        and ple % 8 == 0
        and 2 * ple <= 128
        and sl == sq * n_pts
        and sq % 8 == 0
        and 2 * sl == 128
        and pt % 128 == 0
        and kernel_hat.size < 2**21
    )
    if not fits:
        return plain(
            vectors, kernel_hat, noise_prec, stencil_coefficients_raw, offsets, amplitude, cheb_coef
        )
    forward, inverse = host_tables(length, fb, n_pts, fbp, cfp, tp)
    sizes = (nv, n_sens, n_pts, fb, fbp, cfp, sl, sq, pt, ple, length, tp)
    vmem = pl.BlockSpec(memory_space=pltpu.VMEM)
    smem = pl.BlockSpec(memory_space=pltpu.SMEM)
    anywhere = pl.BlockSpec(memory_space=pl.ANY)

    def f32(*shape):
        return pltpu.VMEM(shape, F32)

    def sems(count):
        return pltpu.SemaphoreType.DMA((count,))

    one = pltpu.SemaphoreType.DMA
    gradient = pl.pallas_call(
        functools.partial(fused_kernel, sizes),
        out_shape=jax.ShapeDtypeStruct(vectors.shape, F32),
        in_specs=[anywhere, anywhere, smem, vmem, vmem, vmem, smem, anywhere, anywhere],
        out_specs=vmem,
        scratch_shapes=[
            pltpu.VMEM(forward.shape, BF),
            pltpu.VMEM(inverse.shape, BF),
            f32(2, fb, sl, pt),
            pltpu.VMEM((fbp, 4 * sl, pt), BF),
            pltpu.VMEM((fbp, pt, 4 * sl), BF),
            f32(nv, ple, length),
            f32(nv, ple, tp),
            f32(n_pts, ple + 8, cfp),
            f32(n_pts, ple + 8, cfp),
            f32(2, nv, ple, cfp),
            f32(nv, n_pts, ple, cfp),
            f32(2, nv, fbp, pt),
            f32(fbp // 8, 2 * nv, 8, sl),
            f32(n_pts, nv, sq, cfp),
            f32(n_pts, nv, sq, cfp),
            f32(n_pts, nv, sq, cfp),
            f32(n_pts, nv, sq, cfp),
            f32(2, nv, fbp, 2 * sl),
            f32(2, nv, fbp, pt),
            f32(n_sens, 2, fbp, pt),
            f32(n_pts, ple, cfp),
            f32(n_pts, ple, cfp),
            f32(nv, ple, tp),
            sems(4),
            sems(n_pts // 2),
            one,
            sems(n_pts // 2),
            sems(2),
            sems(n_pts // 2),
            one,
            sems(n_sens),
            one,
            sems(n_pts // 2),
            one,
            sems(n_pts // 2),
            one,
            sems(n_sens),
            one,
            sems(n_pts // 2),
            one,
            sems(n_sens),
        ],
        compiler_params=pltpu.CompilerParams(
            collective_id=0, has_side_effects=True, vmem_limit_bytes=56 * 2**20
        ),
    )(
        vectors, kernel_hat, noise_prec, stencil_coefficients_raw.T, offsets.T,
        amplitude.reshape(1, ple), cheb_coef, forward, inverse,
    )
    return vectors + gradient


def solution(mesh):
    placed = (
        P(None, "pts", None),
        P(None, "pts", "sens", None),
        P(("sens", "pts")),
        P("pts", None),
        P("pts", None),
        P("pts"),
        P(),
    )
    return jax.shard_map(
        local, mesh=mesh, in_specs=placed, out_specs=P(None, "pts", None), check_vma=False
    )
```

```python
import functools

import jax
import jax.numpy as jnp
import ml_dtypes
import numpy as np
from jax import lax
from jax.experimental import pallas as pl
from jax.experimental.pallas import tpu as pltpu
from jax.sharding import PartitionSpec as P

exact_evaluation_flag = lax.Precision.HIGHEST


def transform_tables(length, padded):
    time_index = jnp.arange(length, dtype=jnp.int32)
    frequency = jnp.arange(padded, dtype=jnp.int32)
    period = 2 * length
    phase_index = frequency[:, None] * time_index[None, :] % period
    angles = 2.0 * jnp.pi / period * phase_index.astype(jnp.float32)
    active = (frequency <= length).astype(jnp.float32)[:, None]
    cosine = jnp.cos(angles)
    sine_part = jnp.sin(angles)
    forward_operator = jnp.stack([cosine * active, -sine_part * active])
    edge_rows = (frequency == 0) | (frequency == length)
    weight = jnp.where(edge_rows, 1.0, 2.0).astype(jnp.float32)[:, None] * active / period
    inverse = jnp.stack([cosine * weight, -sine_part * weight])
    return (forward_operator, inverse)


def to_spectrum(time_series_values, forward_operator):
    return jnp.einsum(
        "vpt,cft->vcfp", time_series_values, forward_operator, precision=exact_evaluation_flag
    )


def to_series(spectrum, inverse):
    return jnp.einsum("vcfp,cft->vpt", spectrum, inverse, precision=exact_evaluation_flag)


def chebyshev(values_in, operator, cheb_coef):
    previous = values_in
    current = operator(values_in)
    running_sum = cheb_coef[0] * previous + cheb_coef[1] * current
    for degree in range(2, cheb_coef.shape[0]):
        following = 2.0 * operator(current) - previous
        previous, current = (current, following)
        running_sum = running_sum + cheb_coef[degree] * current
    return running_sum


def full_matrix(weights_all, offsets_all):
    point_count = weights_all.shape[0]
    positions = jnp.arange(point_count, dtype=jnp.int32)
    target = positions[:, None] + offsets_all
    dense_operator_matrix = jnp.zeros((point_count, point_count), jnp.float32)
    for column in range(weights_all.shape[1]):
        hit = (target[:, column][:, None] == positions[None, :]).astype(jnp.float32)
        dense_operator_matrix = dense_operator_matrix + weights_all[:, column][:, None] * hit
    return dense_operator_matrix


def plain(vectors, kernel_hat, noise_prec, stencil_coefficients_raw, offsets, amplitude, cheb_coef):
    length = vectors.shape[2]
    freq_block = kernel_hat.shape[1]
    padded = freq_block * lax.axis_size("pts")
    forward_operator, inverse = transform_tables(length, padded)
    weights = stencil_coefficients_raw / jnp.sum(stencil_coefficients_raw, axis=1, keepdims=True)
    kernel_real = kernel_hat[0]
    kernel_imag = kernel_hat[1]
    offsets_all = lax.all_gather(offsets, "pts", axis=0, tiled=True)
    weights_all, amplitude_all = (
        lax.all_gather(weights, "pts", axis=0, tiled=True),
        lax.all_gather(amplitude, "pts", axis=0, tiled=True),
    )
    dense_operator_matrix = full_matrix(weights_all, offsets_all)

    def forward_mean(values):
        return jnp.einsum(
            "vcfq,pq->vcfp", values, dense_operator_matrix, precision=exact_evaluation_flag
        )

    def backward_mean(values):
        return jnp.einsum(
            "vcfp,pq->vcfq", values, dense_operator_matrix, precision=exact_evaluation_flag
        )

    source = to_spectrum(vectors, forward_operator)
    spectrum = lax.all_to_all(source, "pts", split_axis=2, concat_axis=3, tiled=True)
    spectrum = amplitude_all[None, None, None, :] * chebyshev(spectrum, forward_mean, cheb_coef)
    real_part = spectrum[:, 0]
    imag_part = spectrum[:, 1]
    data_real = jnp.einsum(
        "fsp,vfp->vfs", kernel_real, real_part, precision=exact_evaluation_flag
    ) - jnp.einsum("fsp,vfp->vfs", kernel_imag, imag_part, precision=exact_evaluation_flag)
    data_imag = jnp.einsum(
        "fsp,vfp->vfs", kernel_real, imag_part, precision=exact_evaluation_flag
    ) + jnp.einsum("fsp,vfp->vfs", kernel_imag, real_part, precision=exact_evaluation_flag)
    data_spec = jnp.stack([data_real, data_imag], axis=1)
    time_series_values = (
        jnp.einsum(
            "rklu,klq->ruq",
            lax.all_to_all(data_spec, "pts", split_axis=3, concat_axis=2, tiled=True),
            inverse,
            precision=exact_evaluation_flag,
        )
        * noise_prec[None, :, None]
    )
    weighted_result = jnp.einsum(
        "lew,jkw->ljke", time_series_values, forward_operator, precision=exact_evaluation_flag
    )
    weighted_result = lax.all_to_all(
        weighted_result, "pts", split_axis=2, concat_axis=3, tiled=True
    )
    back_real = weighted_result[:, 0]
    back_imag = weighted_result[:, 1]
    grad_real = jnp.einsum(
        "fsp,vfs->vfp", kernel_real, back_real, precision=exact_evaluation_flag
    ) + jnp.einsum("fsp,vfs->vfp", kernel_imag, back_imag, precision=exact_evaluation_flag)
    grad_imag = jnp.einsum(
        "fsp,vfs->vfp", kernel_real, back_imag, precision=exact_evaluation_flag
    ) - jnp.einsum("fsp,vfs->vfp", kernel_imag, back_real, precision=exact_evaluation_flag)
    partial_value = chebyshev(
        amplitude_all[None, None, None, :] * jnp.stack([grad_real, grad_imag], axis=1),
        backward_mean,
        cheb_coef,
    )
    summed = lax.psum(partial_value, "sens")
    moved = lax.all_to_all(summed, "pts", split_axis=3, concat_axis=2, tiled=True)
    gradient = to_series(moved, inverse)
    return vectors + gradient


BF = jnp.bfloat16
F32 = jnp.float32
MESH = pl.DeviceIdType.MESH


def up(size, multiple):
    return -(-size // multiple) * multiple


def host_tables(length, block, blocks, padded_block, lanes, padded_time):
    period = 2 * length
    forward = np.zeros((padded_time, blocks, lanes))
    inverse = np.zeros((blocks, lanes, padded_time))
    time = np.arange(length)
    for index in range(blocks):
        frequency = index * block + np.arange(block)
        angle = 2.0 * np.pi / period * (frequency[:, None] * time[None, :] % period)
        active = (frequency <= length)[:, None]
        edge = (frequency == 0) | (frequency == length)
        weight = np.where(edge, 1.0, 2.0)[:, None] / period
        for part, table in enumerate((np.cos(angle) * active, -np.sin(angle) * active)):
            at = slice(part * padded_block, part * padded_block + block)
            forward[:length, index, at] = table.T
            inverse[index, at, :length] = table * weight
    forward = forward.reshape(padded_time, blocks // 2, 2 * lanes).transpose(1, 0, 2)
    inverse = inverse.reshape(blocks // 2, 2 * lanes, padded_time)
    halves = []
    for table in (forward, inverse):
        high = table.astype(ml_dtypes.bfloat16)
        low = (table - high.astype(np.float64)).astype(ml_dtypes.bfloat16)
        halves.append(np.stack([high, low], axis=1))
    return halves


def split(values):
    high = values.astype(BF)
    return high, (values - high.astype(F32)).astype(BF)


NN = (((1,), (0,)), ((), ()))
NT = (((1,), (1,)), ((), ()))


def dot3(left, right_high, right_low, dims=NN):
    rows = left.shape[0]
    high, low = split(left)
    both = lax.dot_general(
        jnp.concatenate([high, low], axis=0), right_high, dims, preferred_element_type=F32
    )
    cross = lax.dot_general(high, right_low, dims, preferred_element_type=F32)
    return both[:rows] + both[rows:] + cross


def flip(index, step, size):
    flipped, bit = 0, 1
    while bit < size:
        digit = lax.rem(index // bit, 2)
        flipped = flipped + bit * ((1 - digit) if step & bit else digit)
        bit *= 2
    return flipped


def fused_kernel(
    sizes,
    vec, kern, noise, raw, offs, amp, cheb, fwd_in, inv_in,
    out,
    fwd, inv, k_f32, k_hl, v_in, v_pad, a_send, a_recv, b_send, x_all, spec, y_buf,
    d_send, d_recv, e_send, e_recv, l_buf, g_buf, r_recv, h_send, h_recv, o_buf,
    load_sem, k_sem, fwd_sem, a_s, a_r, b_s, b_r, f_s, f_r, d_s, d_r, e_s, e_r, g_s, g_r, h_s, h_r, o_s, o_r,
):
    nv, n_sens, n_pts, fb, fbp, cfp, sl, sq, pt, ple, length, tp = sizes
    me_s = lax.axis_index("sens")
    me_p = lax.axis_index("pts")
    rows = 2 * nv
    pairs = n_pts // 2
    pts_steps = range(1, n_pts)
    sens_steps = range(1, n_sens)
    far_first = list(range(pairs - 1, -1, -1))
    pts_peer = [flip(me_p, step, n_pts) for step in range(n_pts)]
    sens_peer = [flip(me_s, step, n_sens) for step in range(n_sens)]
    pair_peer = [flip(me_p // 2, step, pairs) for step in range(pairs)]

    vec_load = pltpu.make_async_copy(vec, v_in, load_sem.at[0])
    share = -(-fb // n_pts)
    k_spans = [(at, min(share, fb - at)) for at in range(0, fb, share)]
    k_loads = [
        pltpu.make_async_copy(
            kern.at[:, pl.ds(at, count)], k_f32.at[:, pl.ds(at, count)], k_sem.at[index]
        )
        for index, (at, count) in enumerate(k_spans)
    ]
    inv_load = pltpu.make_async_copy(inv_in, inv, load_sem.at[1])
    fwd_loads = [
        pltpu.make_async_copy(fwd_in.at[pair], fwd.at[pair], fwd_sem.at[turn])
        for turn, pair in enumerate(pair_peer)
    ]
    vec_load.start()
    for turn in far_first:
        fwd_loads[turn].start()

    barrier = pltpu.get_barrier_semaphore()
    for step in pts_steps:
        pl.semaphore_signal(
            barrier, inc=1, device_id=(me_s, pts_peer[step]), device_id_type=MESH
        )
    for step in sens_steps:
        pl.semaphore_signal(
            barrier, inc=1, device_id=(sens_peer[step], me_p), device_id_type=MESH
        )

    def to_pts(step, src, dst, send_sem, recv_sem):
        pltpu.make_async_remote_copy(
            src_ref=src, dst_ref=dst, send_sem=send_sem, recv_sem=recv_sem.at[step // 2],
            device_id=(me_s, pts_peer[step]), device_id_type=MESH,
        ).start()

    def to_sens(step, src, dst, send_sem, recv_sem):
        pltpu.make_async_remote_copy(
            src_ref=src, dst_ref=dst, send_sem=send_sem, recv_sem=recv_sem.at[step],
            device_id=(sens_peer[step], me_p), device_id_type=MESH,
        ).start()

    def wait(block, semaphore):
        pltpu.make_async_copy(block, block, semaphore).wait()

    def wait_pair(turn, received, semaphore):
        if turn:
            wait(received.at[pl.ds(2 * pair_peer[turn], 2)], semaphore.at[turn])
        else:
            wait(received.at[pts_peer[1]], semaphore.at[0])

    nb = raw.shape[0]
    raw_t = raw[...]
    pack = jnp.concatenate(
        [
            jnp.concatenate(
                [raw_t / jnp.sum(raw_t, axis=0, keepdims=True), offs[...].astype(F32)], axis=1
            ),
            jnp.concatenate([amp[...], amp[...]], axis=1),
            jnp.zeros((7 - nb, 2 * ple), F32),
        ],
        axis=0,
    )
    for index in range(n_pts):
        a_send[index, ple:] = jnp.zeros((8, cfp), F32)
        a_send[index, ple:, 0 : 2 * ple] = pack

    v_pad[...] = jnp.zeros(v_pad.shape, F32)
    vec_load.wait()
    v_pad[:, :, 0:length] = v_in[...]

    def transformed(values, pair, lines):
        high, low = split(values)
        both = jnp.concatenate([high, low], axis=0)
        part = jnp.dot(both, fwd[pair, 0], preferred_element_type=F32)
        return (
            part[:lines] + part[lines:]
            + jnp.dot(high, fwd[pair, 1], preferred_element_type=F32)
        )

    mine = v_pad[me_s]
    for turn in far_first:
        pair = pair_peer[turn]
        fwd_loads[turn].wait()
        if turn == pairs - 1:
            for load in k_loads:
                load.start()
            inv_load.start()
            pl.semaphore_wait(barrier, n_pts - 1 + n_sens - 1)
        if turn:
            source = transformed(mine, pair, ple)
            for side in range(2):
                a_send[2 * pair + side, 0:ple] = source[:, side * cfp : (side + 1) * cfp]
            for step in (2 * turn, 2 * turn + 1):
                to_pts(step, a_send.at[pts_peer[step]], a_recv.at[me_p], a_s, a_r)
    source = transformed(v_pad[...].reshape(nv * ple, tp), pair_peer[0], nv * ple)
    for side in range(2):
        b_send[side] = source[:, side * cfp : (side + 1) * cfp].reshape(nv, ple, cfp)
    other_side = lax.rem(pts_peer[1], 2)
    to_pts(1, b_send.at[other_side], x_all.at[:, me_p], b_s.at[0], b_r)
    to_pts(1, a_send.at[pts_peer[1], ple:], a_recv.at[me_p, ple:], b_s.at[1], a_r)
    own_side = lax.rem(me_p, 2)
    for v in range(nv):
        x_all[v, me_p] = b_send[own_side, v]
    a_recv[me_p, ple:] = a_send[me_p, ple:]

    def halve(index, carry):
        high, low = split(jnp.concatenate([k_f32[0, index], k_f32[1, index]], axis=0))
        k_hl[index, 0 : 2 * sl] = high
        k_hl[index, 2 * sl : 4 * sl] = low
        return carry

    def halve_span(index):
        at, count = k_spans[index]
        k_loads[index].wait()
        lax.fori_loop(at, at + count, halve, 0, unroll=True)

    for turn in list(range(1, pairs)) + [0]:
        if turn:
            halve_span(turn - 1)
        if turn:
            wait_pair(turn, a_recv, a_r)
            span = pl.ds(2 * pair_peer[turn], 2)
            for step in sens_steps:
                to_sens(
                    step, a_recv.at[span, 0:ple], x_all.at[me_s, span], f_s, f_r
                )
            for side in range(2):
                at = 2 * pair_peer[turn] + side
                x_all[me_s, at] = a_recv[at, 0:ple]
        else:
            wait(a_recv.at[pts_peer[1], ple:], a_r.at[0])
    for index in range(fb, fbp):
        k_hl[index] = jnp.zeros(k_hl.shape[1:], BF)

    gathered = [a_recv[index, ple:] for index in range(n_pts)]
    weights_row = jnp.concatenate([block[:, 0:ple] for block in gathered], axis=1)
    offsets_row = jnp.concatenate([block[:, ple : 2 * ple] for block in gathered], axis=1)
    down = lax.broadcasted_iota(jnp.int32, (pt, pt), 0)
    across = lax.broadcasted_iota(jnp.int32, (pt, pt), 1)
    shift = (down - across).astype(F32)
    mean_t = jnp.zeros((pt, pt), F32)
    for k in range(nb):
        mean_t = mean_t + jnp.where(
            shift == offsets_row[k : k + 1], weights_row[k : k + 1], 0.0
        )
    identity = jnp.where(down == across, 1.0, 0.0).astype(F32)
    before, now = identity, mean_t
    total = cheb[0] * before + cheb[1] * now
    mean_h, mean_l = split(mean_t)
    for degree in range(2, cheb.shape[0]):
        before, now = now, 2.0 * dot3(now, mean_h, mean_l) - before
        total = total + cheb[degree] * now
    prior_t = total * weights_row[nb : nb + 1]
    prior_h, prior_l = split(prior_t)

    wait(x_all.at[:, pts_peer[1]], b_r.at[0])
    for other in range(n_sens):
        v = sens_peer[other]
        if other == 1:
            for index in range(pairs - 1, len(k_spans)):
                halve_span(index)
        if other:
            wait(x_all.at[v, pl.ds(0, n_pts - 2)], f_r.at[other])
        own = dot3(jnp.transpose(x_all[v].reshape(pt, cfp)), prior_h, prior_l)
        for part in range(2):
            spec[part, v] = own[part * fbp : (part + 1) * fbp]

    lane = lax.broadcasted_iota(jnp.int32, (1, 16 * rows), 1)
    lane_of = lax.rem(lane, 8)
    sign = jnp.where(lax.rem(lane // (8 * nv), 2) == 0, -1.0, 1.0).astype(F32)

    def columns(values):
        high = values.astype(BF).astype(F32)
        return jnp.transpose(jnp.concatenate([high, values - high], axis=0)).astype(BF)

    def keep_own(products):
        kept = products[0]
        for index in range(1, 8):
            kept = jnp.where(lane_of == index, products[index], kept)
        return kept + pltpu.roll(kept, 8 * rows, 1)

    for group in range(fbp // 8):
        at = 8 * group
        weight = columns(
            jnp.concatenate(
                [spec[part, v, at : at + 8] for part in range(2) for v in range(nv)], axis=0
            )
        )
        product = jnp.dot(
            k_hl[at : at + 8].reshape(32 * sl, pt), weight, preferred_element_type=F32
        ).reshape(8, 2, 2 * sl, 16 * rows)
        kept = keep_own([product[index, 0] + product[index, 1] for index in range(8)])
        data = kept[:sl] + sign * pltpu.roll(kept[sl:], 8 * nv, 1)
        y_buf[group] = jnp.transpose(data)[: 8 * rows].reshape(rows, 8, sl)

    blank = jnp.zeros((cfp - 2 * fbp, sl), F32)
    for v in range(nv):
        data = jnp.transpose(
            jnp.concatenate(
                [y_buf[group, part * nv + v] for part in range(2) for group in range(fbp // 8)]
                + [blank],
                axis=0,
            )
        )
        for index in range(n_pts):
            d_send[index, v] = data[index * sq : (index + 1) * sq]
    for step in reversed(pts_steps):
        to_pts(step, d_send.at[pts_peer[step]], d_recv.at[me_p], d_s, d_r)
    d_recv[me_p] = d_send[me_p]
    inv_load.wait()
    which = lax.rem(lax.broadcasted_iota(jnp.int32, (nv * sq, 1), 0), sq)
    precision = jnp.zeros((nv * sq, 1), F32)
    for index in range(sq):
        precision = jnp.where(which == index, noise[index], precision)

    def series(received, lines, recv_sem):
        result = jnp.zeros((lines, tp), F32)
        for turn in range(pairs):
            wait_pair(turn, received, recv_sem)
            pair = pair_peer[turn]
            both = jnp.concatenate(
                [received[2 * pair + side].reshape(lines, cfp) for side in range(2)], axis=1
            )
            result = result + dot3(both, inv[pair, 0], inv[pair, 1])
        return result

    data = series(d_recv, nv * sq, d_r) * precision
    for turn in far_first:
        pair = pair_peer[turn]
        back = transformed(data, pair, nv * sq)
        for side in range(2):
            e_send[2 * pair + side] = back[:, side * cfp : (side + 1) * cfp].reshape(nv, sq, cfp)
        for step in (2 * turn + 1, 2 * turn):
            if step:
                to_pts(step, e_send.at[pts_peer[step]], e_recv.at[me_p], e_s, e_r)
    e_recv[me_p] = e_send[me_p]
    for turn in range(pairs):
        wait_pair(turn, e_recv, e_r)
    for v in range(nv):
        turned = jnp.transpose(
            jnp.concatenate([e_recv[index, v] for index in range(n_pts)], axis=0)
        )
        real, imag = turned[:fbp], turned[fbp : 2 * fbp]
        l_buf[0, v] = jnp.concatenate([real, imag], axis=1)
        l_buf[1, v] = jnp.concatenate([imag, -real], axis=1)

    tiles = pt // 128
    l_rows = l_buf.reshape(rows * fbp, 2 * sl)
    g_rows = g_buf.reshape(rows * tiles * fbp, 128)

    def adjoint(index, carry):
        high, low = split(l_rows[pl.ds(index, rows, stride=fbp), :])
        left = jnp.concatenate(
            [
                jnp.concatenate([high, high], axis=1),
                jnp.concatenate([low, jnp.zeros_like(low)], axis=1),
            ],
            axis=0,
        )
        product = jnp.dot(left, k_hl[index], preferred_element_type=F32)
        result = product[:rows] + product[rows:]
        for tile in range(tiles):
            g_rows[pl.ds(tile * fbp + index, rows, stride=tiles * fbp), :] = result[
                :, tile * 128 : (tile + 1) * 128
            ]
        return carry

    groups = [(at, min(24, fbp - at)) for at in range(0, fbp, 24)]
    for at, count in groups:
        lax.fori_loop(at, at + count, adjoint, 0, unroll=8)
        for step in reversed(sens_steps):
            to_sens(
                step,
                g_buf.at[:, sens_peer[step], :, pl.ds(at, count), :],
                r_recv.at[me_s, :, :, pl.ds(at, count), :],
                g_s, g_r,
            )
    gradient = g_buf[:, me_s]
    for step in sens_steps:
        wait(r_recv.at[sens_peer[step]], g_r.at[step])
        gradient = gradient + r_recv[sens_peer[step]]
    gradient = jnp.concatenate(
        [
            jnp.concatenate([gradient[part, tile] for tile in range(tiles)], axis=1)
            for part in range(2)
        ]
        + [jnp.zeros((cfp - 2 * fbp, pt), F32)],
        axis=0,
    )
    grad_h, grad_l = split(gradient)
    h_send[...] = dot3(prior_t, grad_h, grad_l, NT).reshape(h_send.shape)
    for step in reversed(pts_steps):
        to_pts(step, h_send.at[pts_peer[step]], h_recv.at[me_p], h_s, h_r)
    h_recv[me_p] = h_send[me_p]
    o_buf[me_s] = series(h_recv, ple, h_r)
    for step in reversed(sens_steps):
        to_sens(step, o_buf.at[me_s], o_buf.at[me_s], o_s, o_r)
    out[me_s] = o_buf[me_s, :, 0:length]
    for step in sens_steps:
        wait(o_buf.at[sens_peer[step]], o_r.at[step])
        out[sens_peer[step]] = o_buf[sens_peer[step], :, 0:length]

    wait(a_send.at[pl.ds(0, n_pts - 2)], a_s)
    wait(b_send.at[0], b_s.at[0])
    wait(a_send.at[0, ple:], b_s.at[1])
    wait(x_all.at[pl.ds(0, n_sens - 1), pl.ds(0, n_pts - 2)], f_s)
    for sent, semaphore in ((d_send, d_s), (e_send, e_s), (h_send, h_s)):
        wait(sent.at[pl.ds(0, n_pts - 1)], semaphore)
    wait(r_recv.at[pl.ds(0, n_sens - 1)], g_s)
    wait(o_buf.at[pl.ds(0, n_sens - 1)], o_s)


def local(vectors, kernel_hat, noise_prec, stencil_coefficients_raw, offsets, amplitude, cheb_coef):
    n_sens, n_pts = lax.axis_size("sens"), lax.axis_size("pts")
    nv, ple, length = vectors.shape
    fb, sl, pt = kernel_hat.shape[1:]
    nb = offsets.shape[1]
    fbp = up(fb, 8)
    cfp = up(2 * fbp, 128)
    tp = up(length, 128)
    sq = sl // n_pts
    fits = (
        nv == n_sens
        and 2 * nv == 8
        and n_pts & (n_pts - 1) == 0
        and nb < 8
        and n_pts > 2
        and fb >= n_pts
        and ple % 8 == 0
        and 2 * ple <= 128
        and sl == sq * n_pts
        and sq % 8 == 0
        and 2 * sl == 128
        and pt % 128 == 0
        and kernel_hat.size < 2**21
    )
    if not fits:
        return plain(
            vectors, kernel_hat, noise_prec, stencil_coefficients_raw, offsets, amplitude, cheb_coef
        )
    forward, inverse = host_tables(length, fb, n_pts, fbp, cfp, tp)
    sizes = (nv, n_sens, n_pts, fb, fbp, cfp, sl, sq, pt, ple, length, tp)
    vmem = pl.BlockSpec(memory_space=pltpu.VMEM)
    smem = pl.BlockSpec(memory_space=pltpu.SMEM)
    anywhere = pl.BlockSpec(memory_space=pl.ANY)

    def f32(*shape):
        return pltpu.VMEM(shape, F32)

    def sems(count):
        return pltpu.SemaphoreType.DMA((count,))

    one = pltpu.SemaphoreType.DMA
    gradient = pl.pallas_call(
        functools.partial(fused_kernel, sizes),
        out_shape=jax.ShapeDtypeStruct(vectors.shape, F32),
        in_specs=[anywhere, anywhere, smem, vmem, vmem, vmem, smem, anywhere, anywhere],
        out_specs=vmem,
        scratch_shapes=[
            pltpu.VMEM(forward.shape, BF),
            pltpu.VMEM(inverse.shape, BF),
            f32(2, fb, sl, pt),
            pltpu.VMEM((fbp, 4 * sl, pt), BF),
            f32(nv, ple, length),
            f32(nv, ple, tp),
            f32(n_pts, ple + 8, cfp),
            f32(n_pts, ple + 8, cfp),
            f32(2, nv, ple, cfp),
            f32(nv, n_pts, ple, cfp),
            f32(2, nv, fbp, pt),
            f32(fbp // 8, 2 * nv, 8, sl),
            f32(n_pts, nv, sq, cfp),
            f32(n_pts, nv, sq, cfp),
            f32(n_pts, nv, sq, cfp),
            f32(n_pts, nv, sq, cfp),
            f32(2, nv, fbp, 2 * sl),
            f32(2, nv, pt // 128, fbp, 128),
            f32(n_sens, 2, pt // 128, fbp, 128),
            f32(n_pts, ple, cfp),
            f32(n_pts, ple, cfp),
            f32(nv, ple, tp),
            sems(2),
            sems(n_pts),
            sems(n_pts // 2),
            one,
            sems(n_pts // 2),
            sems(2),
            sems(n_pts // 2),
            one,
            sems(n_sens),
            one,
            sems(n_pts // 2),
            one,
            sems(n_pts // 2),
            one,
            sems(n_sens),
            one,
            sems(n_pts // 2),
            one,
            sems(n_sens),
        ],
        compiler_params=pltpu.CompilerParams(
            collective_id=0, has_side_effects=True, vmem_limit_bytes=56 * 2**20
        ),
    )(
        vectors, kernel_hat, noise_prec, stencil_coefficients_raw.T, offsets.T,
        amplitude.reshape(1, ple), cheb_coef, forward, inverse,
    )
    return vectors + gradient


def solution(mesh):
    placed = (
        P(None, "pts", None),
        P(None, "pts", "sens", None),
        P(("sens", "pts")),
        P("pts", None),
        P("pts", None),
        P("pts"),
        P(),
    )
    return jax.shard_map(
        local, mesh=mesh, in_specs=placed, out_specs=P(None, "pts", None), check_vma=False
    )
```

```python
import functools

import jax
import jax.numpy as jnp
import ml_dtypes
import numpy as np
from jax import lax
from jax.experimental import pallas as pl
from jax.experimental.pallas import tpu as pltpu
from jax.sharding import PartitionSpec as P

exact_evaluation_flag = lax.Precision.HIGHEST


def transform_tables(length, padded):
    time_index = jnp.arange(length, dtype=jnp.int32)
    frequency = jnp.arange(padded, dtype=jnp.int32)
    period = 2 * length
    phase_index = frequency[:, None] * time_index[None, :] % period
    angles = 2.0 * jnp.pi / period * phase_index.astype(jnp.float32)
    active = (frequency <= length).astype(jnp.float32)[:, None]
    cosine = jnp.cos(angles)
    sine_part = jnp.sin(angles)
    forward_operator = jnp.stack([cosine * active, -sine_part * active])
    edge_rows = (frequency == 0) | (frequency == length)
    weight = jnp.where(edge_rows, 1.0, 2.0).astype(jnp.float32)[:, None] * active / period
    inverse = jnp.stack([cosine * weight, -sine_part * weight])
    return (forward_operator, inverse)


def to_spectrum(time_series_values, forward_operator):
    return jnp.einsum(
        "vpt,cft->vcfp", time_series_values, forward_operator, precision=exact_evaluation_flag
    )


def to_series(spectrum, inverse):
    return jnp.einsum("vcfp,cft->vpt", spectrum, inverse, precision=exact_evaluation_flag)


def chebyshev(values_in, operator, cheb_coef):
    previous = values_in
    current = operator(values_in)
    running_sum = cheb_coef[0] * previous + cheb_coef[1] * current
    for degree in range(2, cheb_coef.shape[0]):
        following = 2.0 * operator(current) - previous
        previous, current = (current, following)
        running_sum = running_sum + cheb_coef[degree] * current
    return running_sum


def full_matrix(weights_all, offsets_all):
    point_count = weights_all.shape[0]
    positions = jnp.arange(point_count, dtype=jnp.int32)
    target = positions[:, None] + offsets_all
    dense_operator_matrix = jnp.zeros((point_count, point_count), jnp.float32)
    for column in range(weights_all.shape[1]):
        hit = (target[:, column][:, None] == positions[None, :]).astype(jnp.float32)
        dense_operator_matrix = dense_operator_matrix + weights_all[:, column][:, None] * hit
    return dense_operator_matrix


def plain(vectors, kernel_hat, noise_prec, stencil_coefficients_raw, offsets, amplitude, cheb_coef):
    length = vectors.shape[2]
    freq_block = kernel_hat.shape[1]
    padded = freq_block * lax.axis_size("pts")
    forward_operator, inverse = transform_tables(length, padded)
    weights = stencil_coefficients_raw / jnp.sum(stencil_coefficients_raw, axis=1, keepdims=True)
    kernel_real = kernel_hat[0]
    kernel_imag = kernel_hat[1]
    offsets_all = lax.all_gather(offsets, "pts", axis=0, tiled=True)
    weights_all, amplitude_all = (
        lax.all_gather(weights, "pts", axis=0, tiled=True),
        lax.all_gather(amplitude, "pts", axis=0, tiled=True),
    )
    dense_operator_matrix = full_matrix(weights_all, offsets_all)

    def forward_mean(values):
        return jnp.einsum(
            "vcfq,pq->vcfp", values, dense_operator_matrix, precision=exact_evaluation_flag
        )

    def backward_mean(values):
        return jnp.einsum(
            "vcfp,pq->vcfq", values, dense_operator_matrix, precision=exact_evaluation_flag
        )

    source = to_spectrum(vectors, forward_operator)
    spectrum = lax.all_to_all(source, "pts", split_axis=2, concat_axis=3, tiled=True)
    spectrum = amplitude_all[None, None, None, :] * chebyshev(spectrum, forward_mean, cheb_coef)
    real_part = spectrum[:, 0]
    imag_part = spectrum[:, 1]
    data_real = jnp.einsum(
        "fsp,vfp->vfs", kernel_real, real_part, precision=exact_evaluation_flag
    ) - jnp.einsum("fsp,vfp->vfs", kernel_imag, imag_part, precision=exact_evaluation_flag)
    data_imag = jnp.einsum(
        "fsp,vfp->vfs", kernel_real, imag_part, precision=exact_evaluation_flag
    ) + jnp.einsum("fsp,vfp->vfs", kernel_imag, real_part, precision=exact_evaluation_flag)
    data_spec = jnp.stack([data_real, data_imag], axis=1)
    time_series_values = (
        jnp.einsum(
            "rklu,klq->ruq",
            lax.all_to_all(data_spec, "pts", split_axis=3, concat_axis=2, tiled=True),
            inverse,
            precision=exact_evaluation_flag,
        )
        * noise_prec[None, :, None]
    )
    weighted_result = jnp.einsum(
        "lew,jkw->ljke", time_series_values, forward_operator, precision=exact_evaluation_flag
    )
    weighted_result = lax.all_to_all(
        weighted_result, "pts", split_axis=2, concat_axis=3, tiled=True
    )
    back_real = weighted_result[:, 0]
    back_imag = weighted_result[:, 1]
    grad_real = jnp.einsum(
        "fsp,vfs->vfp", kernel_real, back_real, precision=exact_evaluation_flag
    ) + jnp.einsum("fsp,vfs->vfp", kernel_imag, back_imag, precision=exact_evaluation_flag)
    grad_imag = jnp.einsum(
        "fsp,vfs->vfp", kernel_real, back_imag, precision=exact_evaluation_flag
    ) - jnp.einsum("fsp,vfs->vfp", kernel_imag, back_real, precision=exact_evaluation_flag)
    partial_value = chebyshev(
        amplitude_all[None, None, None, :] * jnp.stack([grad_real, grad_imag], axis=1),
        backward_mean,
        cheb_coef,
    )
    summed = lax.psum(partial_value, "sens")
    moved = lax.all_to_all(summed, "pts", split_axis=3, concat_axis=2, tiled=True)
    gradient = to_series(moved, inverse)
    return vectors + gradient


BF = jnp.bfloat16
F32 = jnp.float32
MESH = pl.DeviceIdType.MESH


def up(size, multiple):
    return -(-size // multiple) * multiple


def host_tables(length, block, blocks, padded_block, lanes, padded_time):
    period = 2 * length
    forward = np.zeros((padded_time, blocks, lanes))
    inverse = np.zeros((blocks, lanes, padded_time))
    time = np.arange(length)
    for index in range(blocks):
        frequency = index * block + np.arange(block)
        angle = 2.0 * np.pi / period * (frequency[:, None] * time[None, :] % period)
        active = (frequency <= length)[:, None]
        edge = (frequency == 0) | (frequency == length)
        weight = np.where(edge, 1.0, 2.0)[:, None] / period
        for part, table in enumerate((np.cos(angle) * active, -np.sin(angle) * active)):
            at = slice(part * padded_block, part * padded_block + block)
            forward[:length, index, at] = table.T
            inverse[index, at, :length] = table * weight
    forward = forward.reshape(padded_time, blocks // 2, 2 * lanes).transpose(1, 0, 2)
    inverse = inverse.reshape(blocks // 2, 2 * lanes, padded_time)
    halves = []
    for table in (forward, inverse):
        high = table.astype(ml_dtypes.bfloat16)
        low = (table - high.astype(np.float64)).astype(ml_dtypes.bfloat16)
        halves.append(np.stack([high, low], axis=1))
    return halves


def split(values):
    high = values.astype(BF)
    return high, (values - high.astype(F32)).astype(BF)


NN = (((1,), (0,)), ((), ()))
NT = (((1,), (1,)), ((), ()))


def dot3(left, right_high, right_low, dims=NN):
    rows = left.shape[0]
    high, low = split(left)
    both = lax.dot_general(
        jnp.concatenate([high, low], axis=0), right_high, dims, preferred_element_type=F32
    )
    cross = lax.dot_general(high, right_low, dims, preferred_element_type=F32)
    return both[:rows] + both[rows:] + cross


def flip(index, step, size):
    flipped, bit = 0, 1
    while bit < size:
        digit = lax.rem(index // bit, 2)
        flipped = flipped + bit * ((1 - digit) if step & bit else digit)
        bit *= 2
    return flipped


def fused_kernel(
    sizes,
    vec, kern, noise_in, raw_in, offs_in, amp_in, cheb_in, fwd_in, inv_in,
    out,
    noise, raw, offs, amp, cheb, fwd, inv, k_f32, k_hl, v_in, v_pad, a_send, a_recv, b_send, x_all, spec, y_buf,
    d_send, d_recv, e_send, e_recv, l_buf, g_buf, r_recv, h_send, h_recv, o_buf,
    small_sem, load_sem, k_sem, fwd_sem, a_s, a_r, b_s, b_r, f_s, f_r, d_s, d_r, e_s, e_r, g_s, g_r, h_s, h_r, o_s, o_r,
):
    nv, n_sens, n_pts, fb, fbp, cfp, sl, sq, pt, ple, length, tp = sizes
    me_s = lax.axis_index("sens")
    me_p = lax.axis_index("pts")
    rows = 2 * nv
    pairs = n_pts // 2
    pts_steps = range(1, n_pts)
    sens_steps = range(1, n_sens)
    far_first = list(range(pairs - 1, -1, -1))
    pts_peer = [flip(me_p, step, n_pts) for step in range(n_pts)]
    sens_peer = [flip(me_s, step, n_sens) for step in range(n_sens)]
    pair_peer = [flip(me_p // 2, step, pairs) for step in range(pairs)]

    vec_load = pltpu.make_async_copy(vec, v_in, load_sem.at[0])
    share = -(-fb // n_pts)
    k_spans = [(at, min(share, fb - at)) for at in range(0, fb, share)]
    k_loads = [
        pltpu.make_async_copy(
            kern.at[:, pl.ds(at, count)], k_f32.at[:, pl.ds(at, count)], k_sem.at[index]
        )
        for index, (at, count) in enumerate(k_spans)
    ]
    inv_load = pltpu.make_async_copy(inv_in, inv, load_sem.at[1])
    fwd_loads = [
        pltpu.make_async_copy(fwd_in.at[pair], fwd.at[pair], fwd_sem.at[turn])
        for turn, pair in enumerate(pair_peer)
    ]
    small_loads = [
        pltpu.make_async_copy(there, here, small_sem.at[index])
        for index, (there, here) in enumerate(
            ((raw_in, raw), (offs_in, offs), (amp_in, amp), (noise_in, noise), (cheb_in, cheb))
        )
    ]
    vec_load.start()
    for load in small_loads:
        load.start()
    for turn in far_first:
        fwd_loads[turn].start()

    barrier = pltpu.get_barrier_semaphore()
    for step in pts_steps:
        pl.semaphore_signal(
            barrier, inc=1, device_id=(me_s, pts_peer[step]), device_id_type=MESH
        )
    for step in sens_steps:
        pl.semaphore_signal(
            barrier, inc=1, device_id=(sens_peer[step], me_p), device_id_type=MESH
        )

    def to_pts(step, src, dst, send_sem, recv_sem):
        pltpu.make_async_remote_copy(
            src_ref=src, dst_ref=dst, send_sem=send_sem, recv_sem=recv_sem.at[step // 2],
            device_id=(me_s, pts_peer[step]), device_id_type=MESH,
        ).start()

    def to_sens(step, src, dst, send_sem, recv_sem):
        pltpu.make_async_remote_copy(
            src_ref=src, dst_ref=dst, send_sem=send_sem, recv_sem=recv_sem.at[step],
            device_id=(sens_peer[step], me_p), device_id_type=MESH,
        ).start()

    def wait(block, semaphore):
        pltpu.make_async_copy(block, block, semaphore).wait()

    def wait_pair(turn, received, semaphore):
        if turn:
            wait(received.at[pl.ds(2 * pair_peer[turn], 2)], semaphore.at[turn])
        else:
            wait(received.at[pts_peer[1]], semaphore.at[0])

    for load in small_loads:
        load.wait()
    nb = raw.shape[0]
    raw_t = raw[...]
    pack = jnp.concatenate(
        [
            jnp.concatenate(
                [raw_t / jnp.sum(raw_t, axis=0, keepdims=True), offs[...].astype(F32)], axis=1
            ),
            jnp.concatenate([amp[...], amp[...]], axis=1),
            jnp.zeros((7 - nb, 2 * ple), F32),
        ],
        axis=0,
    )
    for index in range(n_pts):
        a_send[index, ple:] = jnp.zeros((8, cfp), F32)
        a_send[index, ple:, 0 : 2 * ple] = pack

    v_pad[...] = jnp.zeros(v_pad.shape, F32)
    vec_load.wait()
    v_pad[:, :, 0:length] = v_in[...]

    def transformed(values, pair, lines):
        high, low = split(values)
        both = jnp.concatenate([high, low], axis=0)
        part = jnp.dot(both, fwd[pair, 0], preferred_element_type=F32)
        return (
            part[:lines] + part[lines:]
            + jnp.dot(high, fwd[pair, 1], preferred_element_type=F32)
        )

    mine = v_pad[me_s]
    for turn in far_first:
        pair = pair_peer[turn]
        fwd_loads[turn].wait()
        if turn == pairs - 1:
            for load in k_loads:
                load.start()
            inv_load.start()
            pl.semaphore_wait(barrier, n_pts - 1 + n_sens - 1)
        if turn:
            source = transformed(mine, pair, ple)
            for side in range(2):
                a_send[2 * pair + side, 0:ple] = source[:, side * cfp : (side + 1) * cfp]
            for step in (2 * turn, 2 * turn + 1):
                to_pts(step, a_send.at[pts_peer[step]], a_recv.at[me_p], a_s, a_r)
    source = transformed(v_pad[...].reshape(nv * ple, tp), pair_peer[0], nv * ple)
    for side in range(2):
        b_send[side] = source[:, side * cfp : (side + 1) * cfp].reshape(nv, ple, cfp)
    other_side = lax.rem(pts_peer[1], 2)
    to_pts(1, b_send.at[other_side], x_all.at[:, me_p], b_s.at[0], b_r)
    to_pts(1, a_send.at[pts_peer[1], ple:], a_recv.at[me_p, ple:], b_s.at[1], a_r)
    own_side = lax.rem(me_p, 2)
    for v in range(nv):
        x_all[v, me_p] = b_send[own_side, v]
    a_recv[me_p, ple:] = a_send[me_p, ple:]

    def halve(index, carry):
        high, low = split(jnp.concatenate([k_f32[0, index], k_f32[1, index]], axis=0))
        k_hl[index, 0 : 2 * sl] = high
        k_hl[index, 2 * sl : 4 * sl] = low
        return carry

    def halve_span(index):
        at, count = k_spans[index]
        k_loads[index].wait()
        lax.fori_loop(at, at + count, halve, 0, unroll=True)

    for turn in list(range(1, pairs)) + [0]:
        if turn:
            halve_span(turn - 1)
        if turn:
            wait_pair(turn, a_recv, a_r)
            span = pl.ds(2 * pair_peer[turn], 2)
            for step in sens_steps:
                to_sens(
                    step, a_recv.at[span, 0:ple], x_all.at[me_s, span], f_s, f_r
                )
            for side in range(2):
                at = 2 * pair_peer[turn] + side
                x_all[me_s, at] = a_recv[at, 0:ple]
        else:
            wait(a_recv.at[pts_peer[1], ple:], a_r.at[0])
    for index in range(fb, fbp):
        k_hl[index] = jnp.zeros(k_hl.shape[1:], BF)

    gathered = [a_recv[index, ple:] for index in range(n_pts)]
    weights_row = jnp.concatenate([block[:, 0:ple] for block in gathered], axis=1)
    offsets_row = jnp.concatenate([block[:, ple : 2 * ple] for block in gathered], axis=1)
    down = lax.broadcasted_iota(jnp.int32, (pt, pt), 0)
    across = lax.broadcasted_iota(jnp.int32, (pt, pt), 1)
    shift = (down - across).astype(F32)
    mean_t = jnp.zeros((pt, pt), F32)
    for k in range(nb):
        mean_t = mean_t + jnp.where(
            shift == offsets_row[k : k + 1], weights_row[k : k + 1], 0.0
        )
    identity = jnp.where(down == across, 1.0, 0.0).astype(F32)
    before, now = identity, mean_t
    total = cheb[0] * before + cheb[1] * now
    mean_h, mean_l = split(mean_t)
    for degree in range(2, cheb.shape[0]):
        before, now = now, 2.0 * dot3(now, mean_h, mean_l) - before
        total = total + cheb[degree] * now
    prior_t = total * weights_row[nb : nb + 1]
    prior_h, prior_l = split(prior_t)

    wait(x_all.at[:, pts_peer[1]], b_r.at[0])

    def field_spectra(vectors_now):
        own = dot3(
            jnp.concatenate(
                [jnp.transpose(x_all[v].reshape(pt, cfp)) for v in vectors_now], axis=0
            ),
            prior_h, prior_l,
        )
        for index, v in enumerate(vectors_now):
            for part in range(2):
                at = index * cfp + part * fbp
                spec[part, v] = own[at : at + fbp]

    field_spectra([me_s])
    for index in range(pairs - 1, len(k_spans)):
        halve_span(index)
    for step in sens_steps:
        wait(x_all.at[sens_peer[step], pl.ds(0, n_pts - 2)], f_r.at[step])
    field_spectra(sens_peer[1:])

    lane = lax.broadcasted_iota(jnp.int32, (1, 16 * rows), 1)
    lane_of = lax.rem(lane, 8)
    sign = jnp.where(lax.rem(lane // (8 * nv), 2) == 0, -1.0, 1.0).astype(F32)

    def columns(values):
        high = values.astype(BF).astype(F32)
        return jnp.transpose(jnp.concatenate([high, values - high], axis=0)).astype(BF)

    def keep_own(products):
        kept = products[0]
        for index in range(1, 8):
            kept = jnp.where(lane_of == index, products[index], kept)
        return kept + pltpu.roll(kept, 8 * rows, 1)

    for group in range(fbp // 8):
        at = 8 * group
        weight = columns(
            jnp.concatenate(
                [spec[part, v, at : at + 8] for part in range(2) for v in range(nv)], axis=0
            )
        )
        product = jnp.dot(
            k_hl[at : at + 8].reshape(32 * sl, pt), weight, preferred_element_type=F32
        ).reshape(8, 2, 2 * sl, 16 * rows)
        kept = keep_own([product[index, 0] + product[index, 1] for index in range(8)])
        data = kept[:sl] + sign * pltpu.roll(kept[sl:], 8 * nv, 1)
        y_buf[group] = jnp.transpose(data)[: 8 * rows].reshape(rows, 8, sl)

    blank = jnp.zeros((cfp - 2 * fbp, sl), F32)
    for v in range(nv):
        data = jnp.transpose(
            jnp.concatenate(
                [y_buf[group, part * nv + v] for part in range(2) for group in range(fbp // 8)]
                + [blank],
                axis=0,
            )
        )
        for index in range(n_pts):
            d_send[index, v] = data[index * sq : (index + 1) * sq]
    for step in reversed(pts_steps):
        to_pts(step, d_send.at[pts_peer[step]], d_recv.at[me_p], d_s, d_r)
    d_recv[me_p] = d_send[me_p]
    inv_load.wait()
    which = lax.rem(lax.broadcasted_iota(jnp.int32, (nv * sq, 1), 0), sq)
    precision = jnp.zeros((nv * sq, 1), F32)
    for index in range(sq):
        precision = jnp.where(which == index, noise[index], precision)

    def series(received, lines, recv_sem):
        result = jnp.zeros((lines, tp), F32)
        for turn in range(pairs):
            wait_pair(turn, received, recv_sem)
            pair = pair_peer[turn]
            both = jnp.concatenate(
                [received[2 * pair + side].reshape(lines, cfp) for side in range(2)], axis=1
            )
            result = result + dot3(both, inv[pair, 0], inv[pair, 1])
        return result

    data = series(d_recv, nv * sq, d_r) * precision
    for turn in far_first:
        pair = pair_peer[turn]
        back = transformed(data, pair, nv * sq)
        for side in range(2):
            e_send[2 * pair + side] = back[:, side * cfp : (side + 1) * cfp].reshape(nv, sq, cfp)
        for step in (2 * turn + 1, 2 * turn):
            if step:
                to_pts(step, e_send.at[pts_peer[step]], e_recv.at[me_p], e_s, e_r)
    e_recv[me_p] = e_send[me_p]
    for turn in range(pairs):
        wait_pair(turn, e_recv, e_r)
    for v in range(nv):
        turned = jnp.transpose(
            jnp.concatenate([e_recv[index, v] for index in range(n_pts)], axis=0)
        )
        real, imag = turned[:fbp], turned[fbp : 2 * fbp]
        l_buf[0, v] = jnp.concatenate([real, imag], axis=1)
        l_buf[1, v] = jnp.concatenate([imag, -real], axis=1)

    tiles = pt // 128
    l_rows = l_buf.reshape(rows * fbp, 2 * sl)
    g_rows = g_buf.reshape(rows * tiles * fbp, 128)

    def adjoint(index, carry):
        high, low = split(l_rows[pl.ds(index, rows, stride=fbp), :])
        left = jnp.concatenate(
            [
                jnp.concatenate([high, high], axis=1),
                jnp.concatenate([low, jnp.zeros_like(low)], axis=1),
            ],
            axis=0,
        )
        product = jnp.dot(left, k_hl[index], preferred_element_type=F32)
        result = product[:rows] + product[rows:]
        for tile in range(tiles):
            g_rows[pl.ds(tile * fbp + index, rows, stride=tiles * fbp), :] = result[
                :, tile * 128 : (tile + 1) * 128
            ]
        return carry

    cuts = [0] + list(range(8, fbp, 16)) + [fbp]
    groups = [(at, after - at) for at, after in zip(cuts, cuts[1:])]
    for at, count in groups:
        lax.fori_loop(at, at + count, adjoint, 0, unroll=True)
        for step in reversed(sens_steps):
            to_sens(
                step,
                g_buf.at[:, sens_peer[step], :, pl.ds(at, count), :],
                r_recv.at[me_s, :, :, pl.ds(at, count), :],
                g_s, g_r,
            )
    gradient = g_buf[:, me_s]
    for step in sens_steps:
        wait(r_recv.at[sens_peer[step]], g_r.at[step])
        gradient = gradient + r_recv[sens_peer[step]]
    gradient = jnp.concatenate(
        [
            jnp.concatenate([gradient[part, tile] for tile in range(tiles)], axis=1)
            for part in range(2)
        ]
        + [jnp.zeros((cfp - 2 * fbp, pt), F32)],
        axis=0,
    )
    grad_h, grad_l = split(gradient)
    h_send[...] = dot3(prior_t, grad_h, grad_l, NT).reshape(h_send.shape)
    for step in reversed(pts_steps):
        to_pts(step, h_send.at[pts_peer[step]], h_recv.at[me_p], h_s, h_r)
    h_recv[me_p] = h_send[me_p]
    o_buf[me_s] = series(h_recv, ple, h_r)
    for step in reversed(sens_steps):
        to_sens(step, o_buf.at[me_s], o_buf.at[me_s], o_s, o_r)
    out[me_s] = o_buf[me_s, :, 0:length]
    for step in sens_steps:
        wait(o_buf.at[sens_peer[step]], o_r.at[step])
        out[sens_peer[step]] = o_buf[sens_peer[step], :, 0:length]

    wait(a_send.at[pl.ds(0, n_pts - 2)], a_s)
    wait(b_send.at[0], b_s.at[0])
    wait(a_send.at[0, ple:], b_s.at[1])
    wait(x_all.at[pl.ds(0, n_sens - 1), pl.ds(0, n_pts - 2)], f_s)
    for sent, semaphore in ((d_send, d_s), (e_send, e_s), (h_send, h_s)):
        wait(sent.at[pl.ds(0, n_pts - 1)], semaphore)
    wait(r_recv.at[pl.ds(0, n_sens - 1)], g_s)
    wait(o_buf.at[pl.ds(0, n_sens - 1)], o_s)


def local(vectors, kernel_hat, noise_prec, stencil_coefficients_raw, offsets, amplitude, cheb_coef):
    n_sens, n_pts = lax.axis_size("sens"), lax.axis_size("pts")
    nv, ple, length = vectors.shape
    fb, sl, pt = kernel_hat.shape[1:]
    nb = offsets.shape[1]
    fbp = up(fb, 8)
    cfp = up(2 * fbp, 128)
    tp = up(length, 128)
    sq = sl // n_pts
    fits = (
        nv == n_sens
        and 2 * nv == 8
        and n_pts & (n_pts - 1) == 0
        and nb < 8
        and n_pts > 2
        and fb >= n_pts
        and ple % 8 == 0
        and 2 * ple <= 128
        and sl == sq * n_pts
        and sq % 8 == 0
        and 2 * sl == 128
        and pt % 128 == 0
        and kernel_hat.size < 2**21
    )
    if not fits:
        return plain(
            vectors, kernel_hat, noise_prec, stencil_coefficients_raw, offsets, amplitude, cheb_coef
        )
    forward, inverse = host_tables(length, fb, n_pts, fbp, cfp, tp)
    sizes = (nv, n_sens, n_pts, fb, fbp, cfp, sl, sq, pt, ple, length, tp)
    vmem = pl.BlockSpec(memory_space=pltpu.VMEM)
    anywhere = pl.BlockSpec(memory_space=pl.ANY)

    def f32(*shape):
        return pltpu.VMEM(shape, F32)

    def sems(count):
        return pltpu.SemaphoreType.DMA((count,))

    one = pltpu.SemaphoreType.DMA
    gradient = pl.pallas_call(
        functools.partial(fused_kernel, sizes),
        out_shape=jax.ShapeDtypeStruct(vectors.shape, F32),
        in_specs=[anywhere] * 9,
        out_specs=vmem,
        scratch_shapes=[
            pltpu.SMEM(noise_prec.shape, F32),
            f32(nb, ple),
            pltpu.VMEM((nb, ple), jnp.int32),
            f32(1, ple),
            pltpu.SMEM(cheb_coef.shape, F32),
            pltpu.VMEM(forward.shape, BF),
            pltpu.VMEM(inverse.shape, BF),
            f32(2, fb, sl, pt),
            pltpu.VMEM((fbp, 4 * sl, pt), BF),
            f32(nv, ple, length),
            f32(nv, ple, tp),
            f32(n_pts, ple + 8, cfp),
            f32(n_pts, ple + 8, cfp),
            f32(2, nv, ple, cfp),
            f32(nv, n_pts, ple, cfp),
            f32(2, nv, fbp, pt),
            f32(fbp // 8, 2 * nv, 8, sl),
            f32(n_pts, nv, sq, cfp),
            f32(n_pts, nv, sq, cfp),
            f32(n_pts, nv, sq, cfp),
            f32(n_pts, nv, sq, cfp),
            f32(2, nv, fbp, 2 * sl),
            f32(2, nv, pt // 128, fbp, 128),
            f32(n_sens, 2, pt // 128, fbp, 128),
            f32(n_pts, ple, cfp),
            f32(n_pts, ple, cfp),
            f32(nv, ple, tp),
            sems(5),
            sems(2),
            sems(n_pts),
            sems(n_pts // 2),
            one,
            sems(n_pts // 2),
            sems(2),
            sems(n_pts // 2),
            one,
            sems(n_sens),
            one,
            sems(n_pts // 2),
            one,
            sems(n_pts // 2),
            one,
            sems(n_sens),
            one,
            sems(n_pts // 2),
            one,
            sems(n_sens),
        ],
        compiler_params=pltpu.CompilerParams(
            collective_id=0, has_side_effects=True, vmem_limit_bytes=56 * 2**20
        ),
    )(
        vectors, kernel_hat, noise_prec, stencil_coefficients_raw.T, offsets.T,
        amplitude.reshape(1, ple), cheb_coef, forward, inverse,
    )
    return vectors + gradient


def solution(mesh):
    placed = (
        P(None, "pts", None),
        P(None, "pts", "sens", None),
        P(("sens", "pts")),
        P("pts", None),
        P("pts", None),
        P("pts"),
        P(),
    )
    return jax.shard_map(
        local, mesh=mesh, in_specs=placed, out_specs=P(None, "pts", None), check_vma=False
    )
```

```python
import functools

import jax
import jax.numpy as jnp
import ml_dtypes
import numpy as np
from jax import lax
from jax.experimental import pallas as pl
from jax.experimental.pallas import tpu as pltpu
from jax.sharding import PartitionSpec as P

exact_evaluation_flag = lax.Precision.HIGHEST


def transform_tables(length, padded):
    time_index = jnp.arange(length, dtype=jnp.int32)
    frequency = jnp.arange(padded, dtype=jnp.int32)
    period = 2 * length
    phase_index = frequency[:, None] * time_index[None, :] % period
    angles = 2.0 * jnp.pi / period * phase_index.astype(jnp.float32)
    active = (frequency <= length).astype(jnp.float32)[:, None]
    cosine = jnp.cos(angles)
    sine_part = jnp.sin(angles)
    forward_operator = jnp.stack([cosine * active, -sine_part * active])
    edge_rows = (frequency == 0) | (frequency == length)
    weight = jnp.where(edge_rows, 1.0, 2.0).astype(jnp.float32)[:, None] * active / period
    inverse = jnp.stack([cosine * weight, -sine_part * weight])
    return (forward_operator, inverse)


def to_spectrum(time_series_values, forward_operator):
    return jnp.einsum(
        "vpt,cft->vcfp", time_series_values, forward_operator, precision=exact_evaluation_flag
    )


def to_series(spectrum, inverse):
    return jnp.einsum("vcfp,cft->vpt", spectrum, inverse, precision=exact_evaluation_flag)


def chebyshev(values_in, operator, cheb_coef):
    previous = values_in
    current = operator(values_in)
    running_sum = cheb_coef[0] * previous + cheb_coef[1] * current
    for degree in range(2, cheb_coef.shape[0]):
        following = 2.0 * operator(current) - previous
        previous, current = (current, following)
        running_sum = running_sum + cheb_coef[degree] * current
    return running_sum


def full_matrix(weights_all, offsets_all):
    point_count = weights_all.shape[0]
    positions = jnp.arange(point_count, dtype=jnp.int32)
    target = positions[:, None] + offsets_all
    dense_operator_matrix = jnp.zeros((point_count, point_count), jnp.float32)
    for column in range(weights_all.shape[1]):
        hit = (target[:, column][:, None] == positions[None, :]).astype(jnp.float32)
        dense_operator_matrix = dense_operator_matrix + weights_all[:, column][:, None] * hit
    return dense_operator_matrix


def plain(vectors, kernel_hat, noise_prec, stencil_coefficients_raw, offsets, amplitude, cheb_coef):
    length = vectors.shape[2]
    freq_block = kernel_hat.shape[1]
    padded = freq_block * lax.axis_size("pts")
    forward_operator, inverse = transform_tables(length, padded)
    weights = stencil_coefficients_raw / jnp.sum(stencil_coefficients_raw, axis=1, keepdims=True)
    kernel_real = kernel_hat[0]
    kernel_imag = kernel_hat[1]
    offsets_all = lax.all_gather(offsets, "pts", axis=0, tiled=True)
    weights_all, amplitude_all = (
        lax.all_gather(weights, "pts", axis=0, tiled=True),
        lax.all_gather(amplitude, "pts", axis=0, tiled=True),
    )
    dense_operator_matrix = full_matrix(weights_all, offsets_all)

    def forward_mean(values):
        return jnp.einsum(
            "vcfq,pq->vcfp", values, dense_operator_matrix, precision=exact_evaluation_flag
        )

    def backward_mean(values):
        return jnp.einsum(
            "vcfp,pq->vcfq", values, dense_operator_matrix, precision=exact_evaluation_flag
        )

    source = to_spectrum(vectors, forward_operator)
    spectrum = lax.all_to_all(source, "pts", split_axis=2, concat_axis=3, tiled=True)
    spectrum = amplitude_all[None, None, None, :] * chebyshev(spectrum, forward_mean, cheb_coef)
    real_part = spectrum[:, 0]
    imag_part = spectrum[:, 1]
    data_real = jnp.einsum(
        "fsp,vfp->vfs", kernel_real, real_part, precision=exact_evaluation_flag
    ) - jnp.einsum("fsp,vfp->vfs", kernel_imag, imag_part, precision=exact_evaluation_flag)
    data_imag = jnp.einsum(
        "fsp,vfp->vfs", kernel_real, imag_part, precision=exact_evaluation_flag
    ) + jnp.einsum("fsp,vfp->vfs", kernel_imag, real_part, precision=exact_evaluation_flag)
    data_spec = jnp.stack([data_real, data_imag], axis=1)
    time_series_values = (
        jnp.einsum(
            "rklu,klq->ruq",
            lax.all_to_all(data_spec, "pts", split_axis=3, concat_axis=2, tiled=True),
            inverse,
            precision=exact_evaluation_flag,
        )
        * noise_prec[None, :, None]
    )
    weighted_result = jnp.einsum(
        "lew,jkw->ljke", time_series_values, forward_operator, precision=exact_evaluation_flag
    )
    weighted_result = lax.all_to_all(
        weighted_result, "pts", split_axis=2, concat_axis=3, tiled=True
    )
    back_real = weighted_result[:, 0]
    back_imag = weighted_result[:, 1]
    grad_real = jnp.einsum(
        "fsp,vfs->vfp", kernel_real, back_real, precision=exact_evaluation_flag
    ) + jnp.einsum("fsp,vfs->vfp", kernel_imag, back_imag, precision=exact_evaluation_flag)
    grad_imag = jnp.einsum(
        "fsp,vfs->vfp", kernel_real, back_imag, precision=exact_evaluation_flag
    ) - jnp.einsum("fsp,vfs->vfp", kernel_imag, back_real, precision=exact_evaluation_flag)
    partial_value = chebyshev(
        amplitude_all[None, None, None, :] * jnp.stack([grad_real, grad_imag], axis=1),
        backward_mean,
        cheb_coef,
    )
    summed = lax.psum(partial_value, "sens")
    moved = lax.all_to_all(summed, "pts", split_axis=3, concat_axis=2, tiled=True)
    gradient = to_series(moved, inverse)
    return vectors + gradient


BF = jnp.bfloat16
F32 = jnp.float32
MESH = pl.DeviceIdType.MESH


def up(size, multiple):
    return -(-size // multiple) * multiple


def host_tables(length, block, blocks, padded_block, lanes, padded_time):
    period = 2 * length
    forward = np.zeros((padded_time, blocks, lanes))
    inverse = np.zeros((blocks, lanes, padded_time))
    time = np.arange(length)
    for index in range(blocks):
        frequency = index * block + np.arange(block)
        angle = 2.0 * np.pi / period * (frequency[:, None] * time[None, :] % period)
        active = (frequency <= length)[:, None]
        edge = (frequency == 0) | (frequency == length)
        weight = np.where(edge, 1.0, 2.0)[:, None] / period
        for part, table in enumerate((np.cos(angle) * active, -np.sin(angle) * active)):
            at = slice(part * padded_block, part * padded_block + block)
            forward[:length, index, at] = table.T
            inverse[index, at, :length] = table * weight
    forward = forward.reshape(padded_time, blocks // 2, 2 * lanes).transpose(1, 0, 2)
    inverse = inverse.reshape(blocks // 2, 2 * lanes, padded_time)
    halves = []
    for table in (forward, inverse):
        high = table.astype(ml_dtypes.bfloat16)
        low = (table - high.astype(np.float64)).astype(ml_dtypes.bfloat16)
        halves.append(np.stack([high, low], axis=1))
    return halves


def split(values):
    high = values.astype(BF)
    return high, (values - high.astype(F32)).astype(BF)


NN = (((1,), (0,)), ((), ()))
NT = (((1,), (1,)), ((), ()))


def dot3(left, right_high, right_low, dims=NN):
    rows = left.shape[0]
    high, low = split(left)
    both = lax.dot_general(
        jnp.concatenate([high, low], axis=0), right_high, dims, preferred_element_type=F32
    )
    cross = lax.dot_general(high, right_low, dims, preferred_element_type=F32)
    return both[:rows] + both[rows:] + cross


def flip(index, step, size):
    flipped, bit = 0, 1
    while bit < size:
        digit = lax.rem(index // bit, 2)
        flipped = flipped + bit * ((1 - digit) if step & bit else digit)
        bit *= 2
    return flipped


def fused_kernel(
    sizes,
    vec, kern, noise_in, raw_in, offs_in, amp_in, cheb_in, fwd_in, inv_in,
    out,
    noise, raw, offs, amp, cheb, fwd, inv, k_f32, k_hl, v_in, v_pad, a_send, a_recv, b_send, x_all, spec, y_buf,
    d_send, d_recv, e_send, e_recv, l_buf, g_buf, r_recv, h_send, h_recv, o_buf,
    small_sem, load_sem, k_sem, fwd_sem, a_s, a_r, b_s, b_r, f_s, f_r, d_s, d_r, e_s, e_r, g_s, g_r, h_s, h_r, h_r_late, o_s, o_r,
):
    nv, n_sens, n_pts, fb, fbp, cfp, sl, sq, pt, ple, length, tp = sizes
    me_s = lax.axis_index("sens")
    me_p = lax.axis_index("pts")
    rows = 2 * nv
    pairs = n_pts // 2
    pts_steps = range(1, n_pts)
    sens_steps = range(1, n_sens)
    far_first = list(range(pairs - 1, -1, -1))
    pts_peer = [flip(me_p, step, n_pts) for step in range(n_pts)]
    sens_peer = [flip(me_s, step, n_sens) for step in range(n_sens)]
    pair_peer = [flip(me_p // 2, step, pairs) for step in range(pairs)]

    vec_load = pltpu.make_async_copy(vec, v_in, load_sem.at[0])
    share = -(-fb // n_pts)
    k_spans = [(at, min(share, fb - at)) for at in range(0, fb, share)]
    k_loads = [
        pltpu.make_async_copy(
            kern.at[:, pl.ds(at, count)], k_f32.at[:, pl.ds(at, count)], k_sem.at[index]
        )
        for index, (at, count) in enumerate(k_spans)
    ]
    inv_load = pltpu.make_async_copy(inv_in, inv, load_sem.at[1])
    fwd_loads = [
        pltpu.make_async_copy(fwd_in.at[pair], fwd.at[pair], fwd_sem.at[turn])
        for turn, pair in enumerate(pair_peer)
    ]
    small_loads = [
        pltpu.make_async_copy(there, here, small_sem.at[index])
        for index, (there, here) in enumerate(
            ((raw_in, raw), (offs_in, offs), (amp_in, amp), (noise_in, noise), (cheb_in, cheb))
        )
    ]
    vec_load.start()
    for load in small_loads:
        load.start()
    for turn in far_first:
        fwd_loads[turn].start()

    barrier = pltpu.get_barrier_semaphore()
    for step in pts_steps:
        pl.semaphore_signal(
            barrier, inc=1, device_id=(me_s, pts_peer[step]), device_id_type=MESH
        )
    for step in sens_steps:
        pl.semaphore_signal(
            barrier, inc=1, device_id=(sens_peer[step], me_p), device_id_type=MESH
        )

    def to_pts(step, src, dst, send_sem, recv_sem):
        pltpu.make_async_remote_copy(
            src_ref=src, dst_ref=dst, send_sem=send_sem, recv_sem=recv_sem.at[step // 2],
            device_id=(me_s, pts_peer[step]), device_id_type=MESH,
        ).start()

    def to_sens(step, src, dst, send_sem, recv_sem):
        pltpu.make_async_remote_copy(
            src_ref=src, dst_ref=dst, send_sem=send_sem, recv_sem=recv_sem.at[step],
            device_id=(sens_peer[step], me_p), device_id_type=MESH,
        ).start()

    def wait(block, semaphore):
        pltpu.make_async_copy(block, block, semaphore).wait()

    def wait_pair(turn, received, semaphore, part=slice(None)):
        if turn:
            wait(received.at[pl.ds(2 * pair_peer[turn], 2), part], semaphore.at[turn])
        else:
            wait(received.at[pts_peer[1], part], semaphore.at[0])

    for load in small_loads:
        load.wait()
    nb = raw.shape[0]
    raw_t = raw[...]
    pack = jnp.concatenate(
        [
            jnp.concatenate(
                [raw_t / jnp.sum(raw_t, axis=0, keepdims=True), offs[...].astype(F32)], axis=1
            ),
            jnp.concatenate([amp[...], amp[...]], axis=1),
            jnp.zeros((7 - nb, 2 * ple), F32),
        ],
        axis=0,
    )
    for index in range(n_pts):
        a_send[index, ple:] = jnp.zeros((8, cfp), F32)
        a_send[index, ple:, 0 : 2 * ple] = pack

    v_pad[...] = jnp.zeros(v_pad.shape, F32)
    vec_load.wait()
    v_pad[:, :, 0:length] = v_in[...]

    def transformed(values, pair, lines):
        high, low = split(values)
        both = jnp.concatenate([high, low], axis=0)
        part = jnp.dot(both, fwd[pair, 0], preferred_element_type=F32)
        return (
            part[:lines] + part[lines:]
            + jnp.dot(high, fwd[pair, 1], preferred_element_type=F32)
        )

    mine = v_pad[me_s]
    for turn in far_first:
        pair = pair_peer[turn]
        fwd_loads[turn].wait()
        if turn == pairs - 1:
            for load in k_loads:
                load.start()
            inv_load.start()
            pl.semaphore_wait(barrier, n_pts - 1 + n_sens - 1)
        if turn:
            source = transformed(mine, pair, ple)
            for side in range(2):
                a_send[2 * pair + side, 0:ple] = source[:, side * cfp : (side + 1) * cfp]
            for step in (2 * turn, 2 * turn + 1):
                to_pts(step, a_send.at[pts_peer[step]], a_recv.at[me_p], a_s, a_r)
    source = transformed(v_pad[...].reshape(nv * ple, tp), pair_peer[0], nv * ple)
    for side in range(2):
        b_send[side] = source[:, side * cfp : (side + 1) * cfp].reshape(nv, ple, cfp)
    other_side = lax.rem(pts_peer[1], 2)
    to_pts(1, b_send.at[other_side], x_all.at[:, me_p], b_s.at[0], b_r)
    to_pts(1, a_send.at[pts_peer[1], ple:], a_recv.at[me_p, ple:], b_s.at[1], a_r)
    own_side = lax.rem(me_p, 2)
    for v in range(nv):
        x_all[v, me_p] = b_send[own_side, v]
    a_recv[me_p, ple:] = a_send[me_p, ple:]

    def halve(index, carry):
        high, low = split(jnp.concatenate([k_f32[0, index], k_f32[1, index]], axis=0))
        k_hl[index, 0 : 2 * sl] = high
        k_hl[index, 2 * sl : 4 * sl] = low
        return carry

    def halve_span(index):
        at, count = k_spans[index]
        k_loads[index].wait()
        lax.fori_loop(at, at + count, halve, 0, unroll=True)

    for turn in list(range(1, pairs)) + [0]:
        if turn:
            halve_span(turn - 1)
        if turn:
            wait_pair(turn, a_recv, a_r)
            span = pl.ds(2 * pair_peer[turn], 2)
            for step in sens_steps:
                to_sens(
                    step, a_recv.at[span, 0:ple], x_all.at[me_s, span], f_s, f_r
                )
            for side in range(2):
                at = 2 * pair_peer[turn] + side
                x_all[me_s, at] = a_recv[at, 0:ple]
        else:
            wait(a_recv.at[pts_peer[1], ple:], a_r.at[0])
    for index in range(fb, fbp):
        k_hl[index] = jnp.zeros(k_hl.shape[1:], BF)

    gathered = [a_recv[index, ple:] for index in range(n_pts)]
    weights_row = jnp.concatenate([block[:, 0:ple] for block in gathered], axis=1)
    offsets_row = jnp.concatenate([block[:, ple : 2 * ple] for block in gathered], axis=1)
    down = lax.broadcasted_iota(jnp.int32, (pt, pt), 0)
    across = lax.broadcasted_iota(jnp.int32, (pt, pt), 1)
    shift = (down - across).astype(F32)
    mean_t = jnp.zeros((pt, pt), F32)
    for k in range(nb):
        mean_t = mean_t + jnp.where(
            shift == offsets_row[k : k + 1], weights_row[k : k + 1], 0.0
        )
    identity = jnp.where(down == across, 1.0, 0.0).astype(F32)
    before, now = identity, mean_t
    total = cheb[0] * before + cheb[1] * now
    mean_h, mean_l = split(mean_t)
    for degree in range(2, cheb.shape[0]):
        before, now = now, 2.0 * dot3(now, mean_h, mean_l) - before
        total = total + cheb[degree] * now
    prior_t = total * weights_row[nb : nb + 1]
    prior_h, prior_l = split(prior_t)

    wait(x_all.at[:, pts_peer[1]], b_r.at[0])

    def field_spectra(vectors_now):
        own = dot3(
            jnp.concatenate(
                [jnp.transpose(x_all[v].reshape(pt, cfp)) for v in vectors_now], axis=0
            ),
            prior_h, prior_l,
        )
        for index, v in enumerate(vectors_now):
            for part in range(2):
                at = index * cfp + part * fbp
                spec[part, v] = own[at : at + fbp]

    field_spectra([me_s])
    for index in range(pairs - 1, len(k_spans)):
        halve_span(index)
    for step in sens_steps:
        wait(x_all.at[sens_peer[step], pl.ds(0, n_pts - 2)], f_r.at[step])
    field_spectra(sens_peer[1:])

    lane = lax.broadcasted_iota(jnp.int32, (1, 16 * rows), 1)
    lane_of = lax.rem(lane, 8)
    sign = jnp.where(lax.rem(lane // (8 * nv), 2) == 0, -1.0, 1.0).astype(F32)

    def columns(values):
        high = values.astype(BF).astype(F32)
        return jnp.transpose(jnp.concatenate([high, values - high], axis=0)).astype(BF)

    def keep_own(products):
        kept = products[0]
        for index in range(1, 8):
            kept = jnp.where(lane_of == index, products[index], kept)
        return kept + pltpu.roll(kept, 8 * rows, 1)

    for group in range(fbp // 8):
        at = 8 * group
        weight = columns(
            jnp.concatenate(
                [spec[part, v, at : at + 8] for part in range(2) for v in range(nv)], axis=0
            )
        )
        product = jnp.dot(
            k_hl[at : at + 8].reshape(32 * sl, pt), weight, preferred_element_type=F32
        ).reshape(8, 2, 2 * sl, 16 * rows)
        kept = keep_own([product[index, 0] + product[index, 1] for index in range(8)])
        data = kept[:sl] + sign * pltpu.roll(kept[sl:], 8 * nv, 1)
        y_buf[group] = jnp.transpose(data)[: 8 * rows].reshape(rows, 8, sl)

    blank = jnp.zeros((cfp - 2 * fbp, sl), F32)
    for v in range(nv):
        data = jnp.transpose(
            jnp.concatenate(
                [y_buf[group, part * nv + v] for part in range(2) for group in range(fbp // 8)]
                + [blank],
                axis=0,
            )
        )
        for index in range(n_pts):
            d_send[index, v] = data[index * sq : (index + 1) * sq]
    for step in reversed(pts_steps):
        to_pts(step, d_send.at[pts_peer[step]], d_recv.at[me_p], d_s, d_r)
    d_recv[me_p] = d_send[me_p]
    inv_load.wait()
    which = lax.rem(lax.broadcasted_iota(jnp.int32, (nv * sq, 1), 0), sq)
    precision = jnp.zeros((nv * sq, 1), F32)
    for index in range(sq):
        precision = jnp.where(which == index, noise[index], precision)

    def series(received, lines, recv_sem, part=slice(None)):
        result = jnp.zeros((lines, tp), F32)
        for turn in range(pairs):
            wait_pair(turn, received, recv_sem, part)
            pair = pair_peer[turn]
            both = jnp.concatenate(
                [received[2 * pair + side, part].reshape(lines, cfp) for side in range(2)], axis=1
            )
            result = result + dot3(both, inv[pair, 0], inv[pair, 1])
        return result

    data = series(d_recv, nv * sq, d_r) * precision
    for turn in far_first:
        pair = pair_peer[turn]
        back = transformed(data, pair, nv * sq)
        for side in range(2):
            e_send[2 * pair + side] = back[:, side * cfp : (side + 1) * cfp].reshape(nv, sq, cfp)
        for step in (2 * turn + 1, 2 * turn):
            if step:
                to_pts(step, e_send.at[pts_peer[step]], e_recv.at[me_p], e_s, e_r)
    e_recv[me_p] = e_send[me_p]
    for turn in range(pairs):
        wait_pair(turn, e_recv, e_r)
    for v in range(nv):
        turned = jnp.transpose(
            jnp.concatenate([e_recv[index, v] for index in range(n_pts)], axis=0)
        )
        real, imag = turned[:fbp], turned[fbp : 2 * fbp]
        l_buf[0, v] = jnp.concatenate([real, imag], axis=1)
        l_buf[1, v] = jnp.concatenate([imag, -real], axis=1)

    tiles = pt // 128
    l_rows = l_buf.reshape(rows * fbp, 2 * sl)
    g_rows = g_buf.reshape(rows * tiles * fbp, 128)

    def adjoint(index, carry):
        high, low = split(l_rows[pl.ds(index, rows, stride=fbp), :])
        left = jnp.concatenate(
            [
                jnp.concatenate([high, high], axis=1),
                jnp.concatenate([low, jnp.zeros_like(low)], axis=1),
            ],
            axis=0,
        )
        product = jnp.dot(left, k_hl[index], preferred_element_type=F32)
        result = product[:rows] + product[rows:]
        for tile in range(tiles):
            g_rows[pl.ds(tile * fbp + index, rows, stride=tiles * fbp), :] = result[
                :, tile * 128 : (tile + 1) * 128
            ]
        return carry

    cuts = [0] + list(range(8, fbp, 16)) + [fbp]
    groups = [(at, after - at) for at, after in zip(cuts, cuts[1:])]
    for at, count in groups:
        lax.fori_loop(at, at + count, adjoint, 0, unroll=True)
        for step in reversed(sens_steps):
            to_sens(
                step,
                g_buf.at[:, sens_peer[step], :, pl.ds(at, count), :],
                r_recv.at[me_s, :, :, pl.ds(at, count), :],
                g_s, g_r,
            )
    gradient = g_buf[:, me_s]
    for step in sens_steps:
        wait(r_recv.at[sens_peer[step]], g_r.at[step])
        gradient = gradient + r_recv[sens_peer[step]]
    gradient = jnp.concatenate(
        [
            jnp.concatenate([gradient[part, tile] for tile in range(tiles)], axis=1)
            for part in range(2)
        ]
        + [jnp.zeros((cfp - 2 * fbp, pt), F32)],
        axis=0,
    )
    grad_h, grad_l = split(gradient)
    h_send[...] = dot3(prior_t, grad_h, grad_l, NT).reshape(h_send.shape)
    halves = [(pl.ds(at, ple // 2), sem) for at, sem in ((0, h_r), (ple // 2, h_r_late))]
    for part, semaphore in halves:
        for step in reversed(pts_steps):
            to_pts(step, h_send.at[pts_peer[step], part], h_recv.at[me_p, part], h_s, semaphore)
    h_recv[me_p] = h_send[me_p]
    for part, semaphore in halves:
        o_buf[me_s, part] = series(h_recv, ple // 2, semaphore, part)
        for step in reversed(sens_steps):
            to_sens(step, o_buf.at[me_s, part], o_buf.at[me_s, part], o_s, o_r)
    out[me_s] = o_buf[me_s, :, 0:length]
    for step in sens_steps:
        wait(o_buf.at[sens_peer[step]], o_r.at[step])
        out[sens_peer[step]] = o_buf[sens_peer[step], :, 0:length]

    wait(a_send.at[pl.ds(0, n_pts - 2)], a_s)
    wait(b_send.at[0], b_s.at[0])
    wait(a_send.at[0, ple:], b_s.at[1])
    wait(x_all.at[pl.ds(0, n_sens - 1), pl.ds(0, n_pts - 2)], f_s)
    for sent, semaphore in ((d_send, d_s), (e_send, e_s), (h_send, h_s)):
        wait(sent.at[pl.ds(0, n_pts - 1)], semaphore)
    wait(r_recv.at[pl.ds(0, n_sens - 1)], g_s)
    wait(o_buf.at[pl.ds(0, n_sens - 1)], o_s)


def local(vectors, kernel_hat, noise_prec, stencil_coefficients_raw, offsets, amplitude, cheb_coef):
    n_sens, n_pts = lax.axis_size("sens"), lax.axis_size("pts")
    nv, ple, length = vectors.shape
    fb, sl, pt = kernel_hat.shape[1:]
    nb = offsets.shape[1]
    fbp = up(fb, 8)
    cfp = up(2 * fbp, 128)
    tp = up(length, 128)
    sq = sl // n_pts
    fits = (
        nv == n_sens
        and 2 * nv == 8
        and n_pts & (n_pts - 1) == 0
        and nb < 8
        and n_pts > 2
        and fb >= n_pts
        and ple % 32 == 0
        and 2 * ple <= 128
        and sl == sq * n_pts
        and sq % 8 == 0
        and 2 * sl == 128
        and pt % 128 == 0
        and kernel_hat.size < 2**21
    )
    if not fits:
        return plain(
            vectors, kernel_hat, noise_prec, stencil_coefficients_raw, offsets, amplitude, cheb_coef
        )
    forward, inverse = host_tables(length, fb, n_pts, fbp, cfp, tp)
    sizes = (nv, n_sens, n_pts, fb, fbp, cfp, sl, sq, pt, ple, length, tp)
    vmem = pl.BlockSpec(memory_space=pltpu.VMEM)
    anywhere = pl.BlockSpec(memory_space=pl.ANY)

    def f32(*shape):
        return pltpu.VMEM(shape, F32)

    def sems(count):
        return pltpu.SemaphoreType.DMA((count,))

    one = pltpu.SemaphoreType.DMA
    gradient = pl.pallas_call(
        functools.partial(fused_kernel, sizes),
        out_shape=jax.ShapeDtypeStruct(vectors.shape, F32),
        in_specs=[anywhere] * 9,
        out_specs=vmem,
        scratch_shapes=[
            pltpu.SMEM(noise_prec.shape, F32),
            f32(nb, ple),
            pltpu.VMEM((nb, ple), jnp.int32),
            f32(1, ple),
            pltpu.SMEM(cheb_coef.shape, F32),
            pltpu.VMEM(forward.shape, BF),
            pltpu.VMEM(inverse.shape, BF),
            f32(2, fb, sl, pt),
            pltpu.VMEM((fbp, 4 * sl, pt), BF),
            f32(nv, ple, length),
            f32(nv, ple, tp),
            f32(n_pts, ple + 8, cfp),
            f32(n_pts, ple + 8, cfp),
            f32(2, nv, ple, cfp),
            f32(nv, n_pts, ple, cfp),
            f32(2, nv, fbp, pt),
            f32(fbp // 8, 2 * nv, 8, sl),
            f32(n_pts, nv, sq, cfp),
            f32(n_pts, nv, sq, cfp),
            f32(n_pts, nv, sq, cfp),
            f32(n_pts, nv, sq, cfp),
            f32(2, nv, fbp, 2 * sl),
            f32(2, nv, pt // 128, fbp, 128),
            f32(n_sens, 2, pt // 128, fbp, 128),
            f32(n_pts, ple, cfp),
            f32(n_pts, ple, cfp),
            f32(nv, ple, tp),
            sems(5),
            sems(2),
            sems(n_pts),
            sems(n_pts // 2),
            one,
            sems(n_pts // 2),
            sems(2),
            sems(n_pts // 2),
            one,
            sems(n_sens),
            one,
            sems(n_pts // 2),
            one,
            sems(n_pts // 2),
            one,
            sems(n_sens),
            one,
            sems(n_pts // 2),
            sems(n_pts // 2),
            one,
            sems(n_sens),
        ],
        compiler_params=pltpu.CompilerParams(
            collective_id=0, has_side_effects=True, vmem_limit_bytes=56 * 2**20
        ),
    )(
        vectors, kernel_hat, noise_prec, stencil_coefficients_raw.T, offsets.T,
        amplitude.reshape(1, ple), cheb_coef, forward, inverse,
    )
    return vectors + gradient


def solution(mesh):
    placed = (
        P(None, "pts", None),
        P(None, "pts", "sens", None),
        P(("sens", "pts")),
        P("pts", None),
        P("pts", None),
        P("pts"),
        P(),
    )
    return jax.shard_map(
        local, mesh=mesh, in_specs=placed, out_specs=P(None, "pts", None), check_vma=False
    )
```
